32 devices in a mesh: row: 4 (over z), col: 8 (over y, x, core).
Axes of the slice: x: 2, y: 2, z: 4, core: 2. Of those that a mesh axis runs over, the one named last changes fastest.
Arguments:
- singles: bfloat16 [512, 384], P('row', 'col'), may hold values from -6 to 6
- pair_in: bfloat16 [512, 512, 128], P('row', 'col'), may hold values from -6 to 6
- proj_weight: bfloat16 [384, 256], P('col'), may hold values from -0.3125 to 0.3125
- gain_first: float32 [128], replicated, may hold values from 0.1 to 1.9
- first_in: bfloat16 [128, 1024], replicated, may hold values from -0.5 to 0.5
- first_out: bfloat16 [512, 128], replicated, may hold values from -0.25 to 0.25
- gain_second: float32 [128], replicated, may hold values from 0.1 to 1.9
- second_in: bfloat16 [128, 1024], replicated, may hold values from -0.5 to 0.5
- second_out: bfloat16 [512, 128], replicated, may hold values from -0.25 to 0.25
- head_weight: bfloat16 [128, 64], replicated, may hold values from -1.5 to 1.5
- pae_bins: int32 [512, 512], P('row', 'col'), may hold values from 0 to 63
- chain_perm: int32 [512], replicated, may hold values from 0 to 511, as said below
- resolved_counts: int32 [4, 8], P('row'), may hold values from 1 to 256, 1024 in all within a row
- tile_order: int32 [4, 2048], P('row', 'col'), may hold values from 0 to 255, as said below
Outputs:
- pair_grad: bfloat16 [512, 512, 128], P('row', 'col')
- single_grad: float32 [512, 384], P('row', 'col')
- second_in_grad: float32 [128, 1024], replicated
- second_out_grad: float32 [512, 128], replicated
- head_grad: float32 [128, 64], replicated
The draws below stay inside these ranges and needn't reach their ends.
Inputs may be any that keep to these rules, and one draw needn't show every extreme that they name: chain_perm maps every aligned group of 64 tokens onto itself, moving whole aligned runs of 16 tokens and keeping the order inside a run. Each row of resolved_counts sums to 1024, and its largest entry is 256. In each row of tile_order, entries b * 256 to (b + 1) * 256 - 1 are a permutation of 0 to 255.
All inputs are finite; a program needn't handle non-finite values.
Results may differ from the reference program's by a relative error of at most 0.011.
Values may be sent and summed in bfloat16 or wider, within the bound.
No kernel may reach another device: no remote copies, remote signals or barrier semaphores. Data moves between devices by JAX's collectives and lax.ppermute only.
A program may use at most 64 MiB of HBM per device.

```python
import math
import jax
import jax.numpy as jnp
import numpy as np
from jax import lax

CS = 384
CZ = 128
HID = 512
BINS = 64
TILE = 32
CHAIN = 16
GROUP = 64
R_DEV = 128
C_DEV = 64
N = 512
TILES_DEV = 256
RES_DEV = 128
N_ROW = 4
N_COL = 8


def draw_chain_perm(key, part):
    group_count = N // GROUP
    chain_count = GROUP // CHAIN
    scores = jax.random.randint(key, (group_count, chain_count), 0, 1 << 20) * chain_count + jnp.arange(chain_count, dtype=jnp.int32)[None, :]
    shuffled = jnp.argsort(scores, axis=1).astype(jnp.int32)
    tokens = jnp.arange(group_count, dtype=jnp.int32)[:, None, None] * GROUP + shuffled[:, :, None] * CHAIN + jnp.arange(CHAIN, dtype=jnp.int32)[None, None, :]
    return tokens.reshape(N).astype(jnp.int32)


def draw_tile_order(key, part):
    device_count = N_ROW * N_COL
    scores = jax.random.randint(key, (device_count, TILES_DEV), 0, 1 << 20) * TILES_DEV + jnp.arange(TILES_DEV, dtype=jnp.int32)[None, :]
    ordered = jnp.argsort(scores, axis=1).astype(jnp.int32)
    return ordered.reshape(N_ROW, N_COL * TILES_DEV)


def touch_ends(values, own_key, low, top_value):
    longest = values.shape.index(max(values.shape))
    spots = []
    for shift in (0, 1):
        where = [jax.random.randint(jax.random.fold_in(own_key, axis), (), 0, length) for axis, length in enumerate(values.shape)]
        where[longest] = (where[longest] + shift) % values.shape[longest]
        spots.append(tuple(where))
    return values.at[spots[0]].set(low).at[spots[1]].set(top_value)


def steps_of(rng, dims, split, low, high):
    def one(axis_at, parts):
        heights = jax.random.uniform(jax.random.fold_in(jax.random.fold_in(rng, 6), axis_at), (parts,), jnp.float32, low / len(split), high / len(split))
        return jnp.repeat(jnp.exp(heights), dims[axis_at] // parts).reshape((-1,) + (1,) * (len(dims) - axis_at - 1))

    level = one(*split[0])
    for cut in split[1:]:
        level = level * one(*cut)
    return level


def length_profile(count, total, most, lean):
    weights = [(1 << 20) // math.isqrt(rank ** lean) + 1 for rank in range(2, count + 1)]
    surplus, holding = total - most - (count - 1), [1] * (count - 1)
    while surplus > 0:
        free = [i for i in range(count - 1) if holding[i] < most]
        pool, remaining = sum([weights[i] for i in free]), surplus
        for i in free:
            more = min(most - holding[i], max(1, remaining * weights[i] // pool), surplus)
            holding[i] = holding[i] + more
            surplus = surplus - more
    return np.array([most] + holding)


def uneven_parts(stream_key, number_of, total, bound, slope):
    if number_of == 2:
        one = jax.random.randint(stream_key, (), max(1, total - bound), min(bound, total - 1) + 1)
        return jnp.stack([one, total - one])
    sizes = jnp.asarray(length_profile(number_of, total, bound, slope), jnp.int32)
    pairs = (number_of - 1) // 2
    giver, taker = sizes[1:1 + 2 * pairs:2], sizes[2:2 + 2 * pairs:2]
    room = jnp.minimum(giver - 1, bound - taker)
    shifted = jax.random.randint(jax.random.fold_in(stream_key, 1), (pairs,), 0, 1 << 20) % (room + 1)
    sizes = sizes.at[1:1 + 2 * pairs:2].set(giver - shifted).at[2:2 + 2 * pairs:2].set(taker + shifted)
    return sizes[jax.random.permutation(jax.random.fold_in(stream_key, 2), number_of)]


def bell_draw(rng, shape, scale, limit, split=(), kind=jnp.bfloat16):
    loudness = steps_of(rng, shape, split, -0.22, 0.18) if split else 1.0
    array = jax.random.normal(rng, shape, jnp.float32) * scale * loudness
    return jnp.minimum(jnp.maximum(array, -limit), limit).astype(kind)


def setup_inputs(seed: int = 0) -> dict:
    keys = jax.random.split(jax.random.key(seed), 15)
    singles = bell_draw(keys[0], (N, CS), 1.0, 6.0, ((0, 4), (1, 8)))
    pair_in = bell_draw(keys[1], (N, N, CZ), 1.0, 6.0, ((0, 4), (1, 8)))
    proj_weight = bell_draw(keys[2], (CS, 2 * CZ), CS ** -0.5, 0.3125, ((0, 8),))
    gain_first = jnp.clip(1.0 + 0.18 * jax.random.normal(keys[3], (CZ,), jnp.float32), 0.1, 1.9)
    first_in = bell_draw(keys[4], (CZ, 2 * HID), CZ ** -0.5, 0.5)
    first_out = bell_draw(keys[5], (HID, CZ), HID ** -0.5, 0.25)
    gain_second = jnp.clip(1.0 + 0.18 * jax.random.normal(keys[6], (CZ,), jnp.float32), 0.1, 1.9)
    second_in = bell_draw(keys[7], (CZ, 2 * HID), CZ ** -0.5, 0.5)
    second_out = bell_draw(keys[8], (HID, CZ), HID ** -0.5, 0.25)
    head_weight = bell_draw(keys[9], (CZ, BINS), (CZ // 9) ** -0.5, 1.5)
    pae_bins = touch_ends(jax.random.randint(keys[10], (N, N), 0, BINS), jax.random.fold_in(keys[10], 1), 0, BINS - 1).astype(jnp.int32)
    chain_perm = draw_chain_perm(jax.random.fold_in(keys[14], 71), 0)
    resolved_counts = jax.vmap(lambda own: uneven_parts(own, N_COL, RES_DEV * N_COL, TILES_DEV, 2))(jax.random.split(keys[12], N_ROW)).reshape((N_ROW, N_COL)).astype(jnp.int32)
    tile_order = draw_tile_order(jax.random.fold_in(keys[14], 71), 0)
    return {"singles": singles, "pair_in": pair_in, "proj_weight": proj_weight, "gain_first": gain_first, "first_in": first_in, "first_out": first_out, "gain_second": gain_second, "second_in": second_in, "second_out": second_out, "head_weight": head_weight, "pae_bins": pae_bins, "chain_perm": chain_perm, "resolved_counts": resolved_counts, "tile_order": tile_order}


def contract(left_op, right_op, left_dim, right_dim):
    return lax.dot_general(left_op, right_op, (((left_dim,), (right_dim,)), ((), ())), preferred_element_type=jnp.float32)

def transition_forward(start_z, gain_vec, w_in, w_out):
    hidden_units = w_out.shape[0]
    average = lax.optimization_barrier(jnp.mean(start_z, axis=-1, keepdims=True))
    centred = start_z - average
    scaling = lax.rsqrt(lax.optimization_barrier(jnp.mean(centred * centred, axis=-1, keepdims=True)) + 1e-05)
    normed = centred * scaling
    inputs = (normed * gain_vec).astype(jnp.bfloat16)
    gate_up = jnp.dot(inputs, w_in, preferred_element_type=jnp.float32)
    gate_part = gate_up[:, :hidden_units]
    up_part = gate_up[:, hidden_units:]
    gate_sig = jax.nn.sigmoid(gate_part)
    hidden_act = (gate_part * gate_sig * up_part).astype(jnp.bfloat16)
    result = jnp.dot(hidden_act, w_out, preferred_element_type=jnp.float32)
    return (result, (normed, scaling, inputs, gate_part, up_part, gate_sig, hidden_act))

def transition_backward(saved, grad_out, gain_vec, w_in, w_out, with_weights):
    normed, scaling, inputs, gate_part, up_part, gate_sig, hidden_act = saved
    grad_hidden = contract(grad_out, w_out, 1, 1)
    grad_gate = grad_hidden * up_part * gate_sig * (1.0 + gate_part * (1.0 - gate_sig))
    grad_up = grad_hidden * gate_part * gate_sig
    grad_both = jnp.concatenate([grad_gate, grad_up], axis=1).astype(jnp.bfloat16)
    grad_normed = contract(grad_both, w_in, 1, 1) * gain_vec
    grad_field = scaling * (grad_normed - lax.optimization_barrier(jnp.mean(grad_normed, axis=-1, keepdims=True)) - normed * lax.optimization_barrier(jnp.mean(grad_normed * normed, axis=-1, keepdims=True)))
    if with_weights:
        return (grad_field, contract(inputs, grad_both, 0, 0), contract(hidden_act, grad_out, 0, 0))
    return (grad_field, None, None)

def head_step(rounded_z, targets, keep_mask, head_weight):
    logits = jnp.dot(rounded_z, head_weight, preferred_element_type=jnp.float32)
    exponent = jnp.exp(logits - lax.optimization_barrier(jnp.max(logits, axis=-1, keepdims=True)))
    probability = exponent / lax.optimization_barrier(jnp.sum(exponent, axis=-1, keepdims=True))
    onehot = (targets[:, None] == lax.broadcasted_iota(jnp.int32, logits.shape, 1)).astype(jnp.float32)
    grad_logits = ((probability - onehot) * keep_mask[:, None]).astype(jnp.bfloat16)
    return (contract(grad_logits, head_weight, 1, 1).astype(jnp.bfloat16), contract(rounded_z, grad_logits, 0, 0))

def second_step(pair_one, targets, live_mask, gain_second, second_in, second_out, head_weight):
    start_f = pair_one.astype(jnp.float32)
    delta, saved = transition_forward(start_f, gain_second, second_in, second_out)
    rounded_z = (start_f + live_mask[:, None] * delta).astype(jnp.bfloat16)
    grad_two, head_part = head_step(rounded_z, targets, jnp.ones_like(live_mask), head_weight)
    masked_out = jnp.where(live_mask[:, None] > 0, grad_two, jnp.zeros((), jnp.bfloat16))
    back_field, in_part, out_part = transition_backward(saved, masked_out, gain_second, second_in, second_out, True)
    return ((grad_two.astype(jnp.float32) + back_field).astype(jnp.bfloat16), in_part, out_part, head_part)

def reference(singles, pair_in, proj_weight, gain_first, first_in, first_out, gain_second, second_in, second_out, head_weight, pae_bins, chain_perm, resolved_counts, tile_order):
    projected = jnp.dot(singles, proj_weight, preferred_element_type=jnp.float32)
    left_part = projected[:, :CZ]
    right_round = lax.optimization_barrier(projected[:, CZ:].astype(jnp.bfloat16))
    right_part = right_round.astype(jnp.float32)
    order_grid = tile_order.reshape(N_ROW, N_COL, TILES_DEV)
    rank_grid = jnp.argsort(order_grid, axis=-1).astype(jnp.int32)
    tile_live = (rank_grid < resolved_counts[:, :, None]).reshape(N_ROW, N_COL, R_DEV, C_DEV // TILE)
    tile_live = tile_live.transpose(0, 2, 1, 3).reshape(N, N // TILE)
    pair_live = jnp.repeat(tile_live, TILE, axis=1).astype(jnp.float32)
    targets = pae_bins[chain_perm][:, chain_perm]
    band_rows = 16

    def band_step(running, band_index):
        first_row = band_index * band_rows
        pair_rows = lax.dynamic_slice_in_dim(pair_in, first_row, band_rows, 0).astype(jnp.float32)
        left_rows = lax.dynamic_slice_in_dim(left_part, first_row, band_rows, 0)
        start_z = (pair_rows + left_rows[:, None, :] + right_part[None, :, :]).reshape(band_rows * N, CZ)
        delta, saved_one = transition_forward(start_z, gain_first, first_in, first_out)
        pair_one = (start_z + delta).astype(jnp.bfloat16)
        band_targets = lax.dynamic_slice_in_dim(targets, first_row, band_rows, 0).reshape(band_rows * N)
        band_live = lax.dynamic_slice_in_dim(pair_live, first_row, band_rows, 0).reshape(band_rows * N)
        grad_one, in_part, out_part, head_part = second_step(pair_one, band_targets, band_live, gain_second, second_in, second_out, head_weight)
        back_field, unused_in, unused_out = transition_backward(saved_one, grad_one, gain_first, first_in, first_out, False)
        grad_zero = (grad_one.astype(jnp.float32) + back_field).reshape(band_rows, N, CZ)
        updated = (running[0] + lax.optimization_barrier(jnp.sum(grad_zero, axis=0)), running[1] + in_part, running[2] + out_part, running[3] + head_part)
        return (updated, (grad_zero.astype(jnp.bfloat16), lax.optimization_barrier(jnp.sum(grad_zero, axis=1))))
    initial = (jnp.zeros((N, CZ), jnp.float32), jnp.zeros((CZ, 2 * HID), jnp.float32), jnp.zeros((HID, CZ), jnp.float32), jnp.zeros((CZ, BINS), jnp.float32))
    totals, (pair_bands, left_bands) = lax.scan(band_step, initial, jnp.arange(N // band_rows, dtype=jnp.int32))
    token_grad = jnp.concatenate([left_bands.reshape(N, CZ), totals[0]], axis=1).astype(jnp.bfloat16)
    single_grad = contract(token_grad, proj_weight, 1, 1)
    return (pair_bands.reshape(N, N, CZ), single_grad, totals[1] / N, totals[2] / N, totals[3] / N)
```

```python
import functools

import jax
import jax.numpy as jnp
from jax import lax
from jax.experimental import pallas as pl
from jax.experimental.pallas import tpu as pltpu
from jax.sharding import PartitionSpec as P

TILE = 32
BLOCK_ROWS = 32
CHUNK = 256
F32 = jnp.float32
BF16 = jnp.bfloat16


def dot(left_op, right_op, left_dim=1, right_dim=0):
    return lax.dot_general(
        left_op,
        right_op,
        (((left_dim,), (right_dim,)), ((), ())),
        preferred_element_type=F32,
    )


def norm(field):
    centred = field - jnp.mean(field, axis=-1, keepdims=True)
    scaling = lax.rsqrt(jnp.mean(centred * centred, axis=-1, keepdims=True) + 1e-05)
    return centred * scaling, scaling


def forward(inputs, w_in, w_out, act_ref, slope_ref, hidden_ref):
    hid = w_out.shape[0]
    result = None
    for j in range(0, hid, CHUNK):
        half_gate = dot(inputs, w_in[:, j : j + CHUNK])
        up = dot(inputs, w_in[:, hid + j : hid + j + CHUNK])
        twice_sig = 1.0 + jnp.tanh(half_gate)
        act = half_gate * twice_sig
        hidden = (act * up).astype(BF16)
        act_ref[:, j : j + CHUNK] = act
        slope_ref[:, j : j + CHUNK] = up * (twice_sig + act * (2.0 - twice_sig))
        if hidden_ref is not None:
            hidden_ref[:, j : j + CHUNK] = hidden
        part = dot(hidden, w_out[j : j + CHUNK, :])
        result = part if result is None else result + part
    return result


def backward(grad_out, normed, scaling, gain, w_in, w_out, act_ref, slope_ref, both_ref):
    hid = w_out.shape[0]
    grad_normed = None
    for j in range(0, hid, CHUNK):
        grad_hidden = dot(grad_out, w_out[j : j + CHUNK, :], 1, 1)
        grad_gate = (grad_hidden * slope_ref[:, j : j + CHUNK]).astype(BF16)
        grad_up = (grad_hidden * act_ref[:, j : j + CHUNK]).astype(BF16)
        if both_ref is not None:
            both_ref[:, j : j + CHUNK] = grad_gate
            both_ref[:, hid + j : hid + j + CHUNK] = grad_up
        part = dot(grad_gate, w_in[:, j : j + CHUNK], 1, 1)
        part = part + dot(grad_up, w_in[:, hid + j : hid + j + CHUNK], 1, 1)
        grad_normed = part if grad_normed is None else grad_normed + part
    grad_normed = grad_normed * gain
    mean = jnp.mean(grad_normed, axis=-1, keepdims=True)
    slant = jnp.mean(grad_normed * normed, axis=-1, keepdims=True)
    return scaling * (grad_normed - mean - normed * slant)


def pair_kernel(
    tokens,
    counts_ref,
    order_ref,
    pair_ref,
    left_ref,
    right_ref,
    bins_ref,
    perm_rows_ref,
    perm_cols_ref,
    gain_first_ref,
    first_in_ref,
    first_out_ref,
    gain_second_ref,
    second_in_ref,
    second_out_ref,
    head_ref,
    pair_grad_ref,
    left_grad_ref,
    right_grad_ref,
    weights_ref,
    live_ref,
    target_ref,
    first_half,
    second_half,
    act_one,
    slope_one,
    act_two,
    slope_two,
    hidden_two,
    both_two,
    in_sum,
    out_sum,
    head_sum,
):
    block_rows, cols, width = pair_ref.shape
    pairs = block_rows * cols
    hid = first_out_ref.shape[0]
    tiles = pairs // TILE
    step = pl.program_id(0)
    blocks = target_ref.shape[0]

    @pl.when(step == 0)
    def _():
        right_grad_ref[...] = jnp.zeros_like(right_grad_ref)
        in_sum[...] = jnp.zeros_like(in_sum)
        out_sum[...] = jnp.zeros_like(out_sum)
        head_sum[...] = jnp.zeros_like(head_sum)
        for half, whole in ((first_half, first_in_ref), (second_half, second_in_ref)):
            half[:, :hid] = whole[:, :hid] * jnp.asarray(0.5, BF16)
            half[:, hid:] = whole[:, hid:]
        count = counts_ref[0, lax.axis_index("col")]

        def place(t, carry):
            live_ref[order_ref[0, t]] = jnp.where(t < count, 1.0, 0.0).astype(F32)
            return carry

        lax.fori_loop(0, order_ref.shape[1], place, 0, unroll=8)
        rows = bins_ref.shape[0]
        row_index, col_index = lax.axis_index("row"), lax.axis_index("col")
        perm_rows = perm_rows_ref[pl.ds(row_index, 1), :] - row_index * rows
        perm_cols = perm_cols_ref[pl.ds(col_index, 1), :] - col_index * cols
        pick_rows = (lax.broadcasted_iota(jnp.int32, (rows, rows), 0) == perm_rows).astype(BF16)
        pick_cols = (lax.broadcasted_iota(jnp.int32, (cols, cols), 0) == perm_cols).astype(BF16)
        bins = bins_ref[...].astype(F32).astype(BF16)
        moved = dot(bins, pick_rows, 0, 0).astype(BF16)
        moved = dot(pick_cols, moved, 0, 0)
        for b in range(blocks):
            target_ref[b] = moved[:, b * block_rows : (b + 1) * block_rows].astype(jnp.int32)

    field = pair_ref[...].astype(F32) + left_ref[...][:, None, :]
    field = (field + right_ref[...].astype(F32)[None]).reshape(pairs, width)
    normed_one, scaling_one = norm(field)
    inputs_one = (normed_one * gain_first_ref[...]).astype(BF16)
    delta_one = forward(inputs_one, first_half, first_out_ref, act_one, slope_one, None)
    pair_one = (field + delta_one).astype(BF16).astype(F32)

    normed_two, scaling_two = norm(pair_one)
    inputs_two = (normed_two * gain_second_ref[...]).astype(BF16)
    delta_two = forward(inputs_two, second_half, second_out_ref, act_two, slope_two, hidden_two)
    live = [live_ref[step * tiles + t] for t in range(tiles)]

    def masked(x):
        return jnp.concatenate(
            [x[t * TILE : (t + 1) * TILE] * live[t] for t in range(tiles)], axis=0
        )

    pair_two = (pair_one + masked(delta_two)).astype(BF16)

    logits = dot(pair_two, head_ref[...])
    exponent = jnp.exp(logits - jnp.max(logits, axis=-1, keepdims=True))
    probability = exponent * (1.0 / jnp.sum(exponent, axis=-1, keepdims=True))
    target = target_ref[step]
    bin_ids = lax.broadcasted_iota(jnp.int32, (cols, logits.shape[-1]), 1)
    onehot = jnp.concatenate(
        [(target[:, r : r + 1] == bin_ids).astype(F32) for r in range(block_rows)], axis=0
    )
    grad_logits = (probability - onehot).astype(BF16)
    grad_two = dot(grad_logits, head_ref[...], 1, 1).astype(BF16).astype(F32)
    head_sum[...] += dot(pair_two, grad_logits, 0, 0)

    grad_delta = masked(grad_two).astype(BF16)
    back_two = backward(
        grad_delta,
        normed_two,
        scaling_two,
        gain_second_ref[...],
        second_half,
        second_out_ref,
        act_two,
        slope_two,
        both_two,
    )
    in_sum[...] += dot(inputs_two, both_two[...], 0, 0)
    out_sum[...] += dot(grad_delta, hidden_two[...], 0, 0)

    grad_one = (grad_two + back_two).astype(BF16)
    back_one = backward(
        grad_one,
        normed_one,
        scaling_one,
        gain_first_ref[...],
        first_half,
        first_out_ref,
        act_one,
        slope_one,
        None,
    )
    grad_zero = (grad_one.astype(F32) + back_one).reshape(block_rows, cols, width)
    pair_grad_ref[...] = grad_zero.astype(BF16)
    left_grad_ref[...] = jnp.sum(grad_zero, axis=1)
    right_grad_ref[...] += jnp.sum(grad_zero, axis=0)

    @pl.when(step == pl.num_programs(0) - 1)
    def _():
        scale = 1.0 / tokens
        row = 0
        for j in range(0, 2 * hid, width):
            factor = scale * 0.5 if j < hid else scale
            weights_ref[row : row + width, :] = (in_sum[:, j : j + width] * factor).astype(BF16)
            row += width
        for j in range(0, hid, width):
            part = jnp.transpose(out_sum[:, j : j + width])
            weights_ref[row : row + width, :] = (part * scale).astype(BF16)
            row += width
        half = width // 2
        packed = jnp.concatenate([head_sum[:half, :], head_sum[half:, :]], axis=1) * scale
        weights_ref[row : row + half, :] = packed.astype(BF16)
        row += half
        if row < weights_ref.shape[0]:
            rest = (weights_ref.shape[0] - row, width)
            weights_ref[row:, :] = jnp.zeros(rest, BF16)


def pair_grid(
    counts,
    order,
    pair_in,
    left_part,
    right_part,
    pae_bins,
    perm_rows,
    perm_cols,
    gain_first,
    first_in,
    first_out,
    gain_second,
    second_in,
    second_out,
    head_weight,
    tokens,
    weight_rows,
):
    rows, cols, width = pair_in.shape
    block_rows = min(BLOCK_ROWS, rows)
    pairs = block_rows * cols
    hid = first_out.shape[0]
    bins = head_weight.shape[1]

    def whole(x):
        return pl.BlockSpec(x.shape, lambda i, *_: (0,) * x.ndim)

    def fixed(*shape):
        return pl.BlockSpec(shape, lambda i, *_: (0,) * len(shape))

    small = (
        right_part,
        pae_bins,
        perm_rows,
        perm_cols,
        gain_first,
        first_in,
        first_out,
        gain_second,
        second_in,
        second_out,
        head_weight,
    )
    grid_spec = pltpu.PrefetchScalarGridSpec(
        num_scalar_prefetch=2,
        grid=(rows // block_rows,),
        in_specs=[
            pl.BlockSpec((block_rows, cols, width), lambda i, *_: (i, 0, 0)),
            pl.BlockSpec((block_rows, width), lambda i, *_: (i, 0)),
        ]
        + [whole(x) for x in small],
        out_specs=[
            pl.BlockSpec((block_rows, cols, width), lambda i, *_: (i, 0, 0)),
            pl.BlockSpec((block_rows, width), lambda i, *_: (i, 0)),
            fixed(cols, width),
            fixed(weight_rows, width),
        ],
        scratch_shapes=[
            pltpu.SMEM((rows * cols // TILE,), F32),
            pltpu.VMEM((rows // block_rows, cols, block_rows), jnp.int32),
            pltpu.VMEM((width, 2 * hid), BF16),
            pltpu.VMEM((width, 2 * hid), BF16),
            pltpu.VMEM((pairs, hid), F32),
            pltpu.VMEM((pairs, hid), F32),
            pltpu.VMEM((pairs, hid), F32),
            pltpu.VMEM((pairs, hid), F32),
            pltpu.VMEM((pairs, hid), BF16),
            pltpu.VMEM((pairs, 2 * hid), BF16),
            pltpu.VMEM((width, 2 * hid), F32),
            pltpu.VMEM((width, hid), F32),
            pltpu.VMEM((width, bins), F32),
        ],
    )
    macs = rows * cols * width * (16 * hid + 3 * bins)
    return pl.pallas_call(
        functools.partial(pair_kernel, tokens),
        grid_spec=grid_spec,
        out_shape=[
            jax.ShapeDtypeStruct((rows, cols, width), BF16),
            jax.ShapeDtypeStruct((rows, width), F32),
            jax.ShapeDtypeStruct((cols, width), F32),
            jax.ShapeDtypeStruct((weight_rows, width), BF16),
        ],
        compiler_params=pltpu.CompilerParams(
            vmem_limit_bytes=56 << 20, dimension_semantics=("arbitrary",)
        ),
        cost_estimate=pl.CostEstimate(
            flops=2 * macs,
            bytes_accessed=4 * rows * cols * width,
            transcendentals=2 * rows * cols * hid,
        ),
    )(counts, order, pair_in, left_part, *small)


def swap(x, axis, size, mask):
    return lax.ppermute(x, axis, [(i, i ^ mask) for i in range(size)])


def tree_sum(parts):
    parts = [p.astype(F32) for p in parts]
    while len(parts) > 1:
        parts = [parts[k] + parts[k + 1] for k in range(0, len(parts), 2)]
    return parts[0]


def in_order(parts, index):
    parts = list(parts)
    bit = 1
    while bit < len(parts):
        parts = [
            jnp.where((index & bit) != 0, parts[k ^ bit], parts[k]) for k in range(len(parts))
        ]
        bit *= 2
    return jnp.stack(parts)


def local(
    n_row,
    n_col,
    singles,
    pair_in,
    proj_weight,
    gain_first,
    first_in,
    first_out,
    gain_second,
    second_in,
    second_out,
    head_weight,
    pae_bins,
    chain_perm,
    resolved_counts,
    tile_order,
):
    rows, cols, width = pair_in.shape
    tokens = chain_perm.shape[0]
    hid = first_out.shape[0]
    bins = head_weight.shape[1]
    row_index = lax.axis_index("row")
    col_index = lax.axis_index("col")
    ratio = rows // cols

    joined = jnp.concatenate([singles.T, proj_weight], axis=1)
    joined = lax.all_gather(joined, "col", axis=0, tiled=True)
    projected = dot(joined[:, :rows], joined[:, rows:], 0, 0)
    left_part = projected[:, :width]
    own_half = lax.dynamic_slice_in_dim(
        projected[:, width:], (col_index % ratio) * cols, cols, 0
    ).astype(BF16)
    right_part = lax.ppermute(
        own_half,
        ("row", "col"),
        [
            ((c // ratio) * n_col + z * ratio + c % ratio, z * n_col + c)
            for z in range(n_row)
            for c in range(n_col)
        ],
    )

    used_rows = 3 * hid + width // 2
    share = -(-used_rows // (n_col * 16)) * 16
    pair_grad, left_grad, right_grad, weights = pair_grid(
        resolved_counts,
        tile_order,
        pair_in,
        left_part,
        right_part,
        pae_bins,
        chain_perm.reshape(n_row, rows),
        chain_perm.reshape(n_col, cols),
        gain_first.reshape(1, width),
        first_in,
        first_out,
        gain_second.reshape(1, width),
        second_in,
        second_out,
        head_weight,
        tokens,
        share * n_col,
    )

    right_sent = right_grad.astype(BF16)
    right_parts = [right_sent] + [swap(right_sent, "row", n_row, k) for k in range(1, n_row)]
    right_total = tree_sum(right_parts).astype(BF16)
    spread = [
        lax.ppermute(
            right_total,
            ("row", "col"),
            [
                (z * n_col + c, (c // ratio) * n_col + z * ratio + (p ^ (c % ratio)))
                for z in range(n_row)
                for c in range(n_col)
            ],
        )
        for p in range(ratio)
    ]
    right_tokens = in_order(spread, col_index % ratio).reshape(rows, width)

    left_share = left_grad.astype(BF16).reshape(n_col, rows // n_col, width)
    buffer = jnp.concatenate([weights.reshape(n_col, share, width), left_share], axis=1)
    depth = buffer.shape[1]
    chips = n_col // 2
    chip, core = col_index // 2, col_index % 2
    buffer = buffer.reshape(chips, 2, depth, width)
    kept = lax.dynamic_index_in_dim(buffer, core, 1, keepdims=False)
    sent = lax.dynamic_index_in_dim(buffer, 1 - core, 1, keepdims=False)
    buffer = tree_sum([kept, swap(sent, "col", n_col, 1)]).astype(BF16)
    parts = [lax.dynamic_index_in_dim(buffer, chip, 0, keepdims=False)]
    for k in range(1, chips):
        sent = lax.dynamic_index_in_dim(buffer, chip ^ k, 0, keepdims=False)
        parts.append(swap(sent, "col", n_col, 2 * k))
    buffer = tree_sum(parts).astype(BF16)
    own = buffer[:share]
    own = tree_sum([own] + [swap(own, "row", n_row, k) for k in range(1, n_row)]).astype(BF16)
    buffer = jnp.concatenate([own, buffer[share:]], axis=0)
    buffer = in_order(
        [buffer] + [swap(buffer, "col", n_col, 2 * k) for k in range(1, chips)], chip
    )
    buffer = in_order([buffer, swap(buffer, "col", n_col, 1)], core)
    buffer = buffer.transpose(1, 0, 2, 3).reshape(n_col, depth, width)
    left_tokens = buffer[:, share:].reshape(rows, width)
    weights = buffer[:, :share].reshape(share * n_col, width).astype(F32)

    token_rows = jnp.concatenate([left_tokens, right_tokens], axis=1)
    single_grad = dot(token_rows, proj_weight, 1, 1)
    in_grad = weights[: 2 * hid].reshape(2 * hid // width, width, width)
    in_grad = in_grad.transpose(1, 0, 2).reshape(width, 2 * hid)
    out_grad = weights[2 * hid : 3 * hid]
    head_rows = weights[3 * hid : 3 * hid + width // 2]
    head_grad = jnp.concatenate([head_rows[:, :bins], head_rows[:, bins:]], axis=0)
    return pair_grad, single_grad, in_grad, out_grad, head_grad


def solution(mesh):
    in_specs = (
        P("row", "col"),
        P("row", "col", None),
        P("col", None),
        P(),
        P(),
        P(),
        P(),
        P(),
        P(),
        P(),
        P("row", "col"),
        P(),
        P("row", None),
        P("row", "col"),
    )
    out_specs = (P("row", "col", None), P("row", "col"), P(), P(), P())
    return jax.shard_map(
        functools.partial(local, mesh.shape["row"], mesh.shape["col"]),
        mesh=mesh,
        in_specs=in_specs,
        out_specs=out_specs,
        check_vma=False,
    )
```

```python
import functools

import jax
import jax.numpy as jnp
from jax import lax
from jax.experimental import pallas as pl
from jax.experimental.pallas import tpu as pltpu
from jax.sharding import PartitionSpec as P

TILE = 32
LANES = 128
BLOCK_ROWS = 32
CHUNK = 256
F32 = jnp.float32
BF16 = jnp.bfloat16


def dot(left_op, right_op, left_dim=1, right_dim=0):
    return lax.dot_general(
        left_op,
        right_op,
        (((left_dim,), (right_dim,)), ((), ())),
        preferred_element_type=F32,
    )


def norm(field):
    centred = field - jnp.mean(field, axis=0, keepdims=True)
    scaling = lax.rsqrt(jnp.mean(centred * centred, axis=0, keepdims=True) + 1e-05)
    return centred * scaling, scaling


def forward(inputs, in_turned, out_turned, act_ref, slope_ref, hidden_ref):
    hid = out_turned.shape[1]
    result = None
    for j in range(0, hid, CHUNK):
        half_gate = dot(in_turned[j : j + CHUNK, :], inputs).astype(BF16)
        up = dot(in_turned[hid + j : hid + j + CHUNK, :], inputs).astype(BF16)
        twice_sig = 1.0 + jnp.tanh(half_gate)
        act = half_gate * twice_sig
        hidden = act * up
        act_ref[j : j + CHUNK, :] = act
        slope_ref[j : j + CHUNK, :] = up * (twice_sig + act * (2.0 - twice_sig))
        if hidden_ref is not None:
            hidden_ref[j : j + CHUNK, :] = hidden
        part = dot(out_turned[:, j : j + CHUNK], hidden)
        result = part if result is None else result + part
    return result


def backward(grad_out, normed, scaling, gain, w_in, w_out, act_ref, slope_ref, both_ref):
    hid = w_out.shape[0]
    grad_normed = None
    for j in range(0, hid, CHUNK):
        grad_hidden = dot(w_out[j : j + CHUNK, :], grad_out).astype(BF16)
        grad_gate = grad_hidden * slope_ref[j : j + CHUNK, :]
        grad_up = grad_hidden * act_ref[j : j + CHUNK, :]
        if both_ref is not None:
            both_ref[j : j + CHUNK, :] = grad_gate
            both_ref[hid + j : hid + j + CHUNK, :] = grad_up
        part = dot(w_in[:, j : j + CHUNK], grad_gate)
        part = part + dot(w_in[:, hid + j : hid + j + CHUNK], grad_up)
        grad_normed = part if grad_normed is None else grad_normed + part
    grad_normed = grad_normed * gain
    mean = jnp.mean(grad_normed, axis=0, keepdims=True)
    slant = jnp.mean(grad_normed * normed, axis=0, keepdims=True)
    return scaling * (grad_normed - mean - normed * slant)


def turned(x):
    return jnp.transpose(x.astype(F32)).astype(x.dtype)


def pair_kernel(
    tokens,
    counts_ref,
    order_ref,
    pair_ref,
    left_ref,
    right_ref,
    bins_ref,
    perm_rows_ref,
    perm_cols_ref,
    gain_first_ref,
    first_in_ref,
    first_out_ref,
    gain_second_ref,
    second_in_ref,
    second_out_ref,
    head_ref,
    pair_grad_ref,
    left_grad_ref,
    right_grad_ref,
    weights_ref,
    live_ref,
    target_ref,
    rows_ref,
    gains_ref,
    first_half,
    second_half,
    first_in_turned,
    second_in_turned,
    first_out_turned,
    second_out_turned,
    head_turned,
    act_one,
    slope_one,
    act_two,
    slope_two,
    hidden_two,
    both_two,
    in_sum,
    out_sum,
    head_sum,
):
    block_rows, cols, width = pair_ref.shape
    pairs = block_rows * cols
    hid = first_out_ref.shape[0]
    step = pl.program_id(0)
    group = LANES // cols
    vectors = pairs // LANES

    @pl.when(step == 0)
    def _():
        right_grad_ref[...] = jnp.zeros_like(right_grad_ref)
        in_sum[...] = jnp.zeros_like(in_sum)
        out_sum[...] = jnp.zeros_like(out_sum)
        head_sum[...] = jnp.zeros_like(head_sum)
        for half, half_turned, whole in (
            (first_half, first_in_turned, first_in_ref),
            (second_half, second_in_turned, second_in_ref),
        ):
            half[:, :hid] = whole[:, :hid] * jnp.asarray(0.5, BF16)
            half[:, hid:] = whole[:, hid:]
            half_turned[...] = turned(half[...])
        first_out_turned[...] = turned(first_out_ref[...])
        second_out_turned[...] = turned(second_out_ref[...])
        head_turned[...] = turned(head_ref[...])
        gains_ref[:, 0:1] = jnp.transpose(gain_first_ref[...])
        gains_ref[:, 1:2] = jnp.transpose(gain_second_ref[...])
        count = counts_ref[0, lax.axis_index("col")]

        def place(t, carry):
            live_ref[order_ref[0, t]] = jnp.where(t < count, 1.0, 0.0).astype(F32)
            return carry

        lax.fori_loop(0, order_ref.shape[1], place, 0, unroll=8)
        rows = bins_ref.shape[0]
        row_index, col_index = lax.axis_index("row"), lax.axis_index("col")
        perm_rows = perm_rows_ref[pl.ds(row_index, 1), :] - row_index * rows
        perm_cols = perm_cols_ref[pl.ds(col_index, 1), :] - col_index * cols
        pick_rows = (lax.broadcasted_iota(jnp.int32, (rows, rows), 0) == perm_rows).astype(BF16)
        pick_cols = (lax.broadcasted_iota(jnp.int32, (cols, cols), 0) == perm_cols).astype(BF16)
        bins = bins_ref[...].astype(F32).astype(BF16)
        moved = dot(pick_rows, bins, 0, 0).astype(BF16)
        rows_ref[...] = dot(moved, pick_cols)
        target_ref[...] = jnp.concatenate(
            [rows_ref[pl.ds(k, rows // group, stride=group), :] for k in range(group)], axis=1
        )

    field = pair_ref[...].astype(F32) + left_ref[...][:, None, :]
    field = (field + right_ref[...].astype(F32)[None]).reshape(pairs, width)
    field = jnp.transpose(field)
    normed_one, scaling_one = norm(field)
    inputs_one = (normed_one * gains_ref[:, 0:1]).astype(BF16)
    delta_one = forward(inputs_one, first_in_turned, first_out_turned, act_one, slope_one, None)
    pair_one = (field + delta_one).astype(BF16).astype(F32)

    normed_two, scaling_two = norm(pair_one)
    inputs_two = (normed_two * gains_ref[:, 1:2]).astype(BF16)
    delta_two = forward(
        inputs_two, second_in_turned, second_out_turned, act_two, slope_two, hidden_two
    )
    lane_tile = lax.broadcasted_iota(jnp.int32, (1, LANES), 1) // TILE
    tiles = LANES // TILE
    live_parts = []
    for k in range(vectors):
        first_tile = (step * vectors + k) * tiles
        part = jnp.full((1, LANES), live_ref[first_tile], F32)
        for t in range(1, tiles):
            part = jnp.where(lane_tile == t, live_ref[first_tile + t], part)
        live_parts.append(part)
    live = jnp.concatenate(live_parts, axis=1)
    pair_two = (pair_one + live * delta_two).astype(BF16)

    logits = dot(head_turned[...], pair_two)
    exponent = jnp.exp(logits - jnp.max(logits, axis=0, keepdims=True))
    probability = exponent * (1.0 / jnp.sum(exponent, axis=0, keepdims=True))
    target = jnp.concatenate(
        [target_ref[pl.ds(step * vectors + k, 1), :] for k in range(vectors)], axis=1
    ).astype(jnp.int32)
    onehot = lax.broadcasted_iota(jnp.int32, logits.shape, 0) == target
    grad_logits = (probability - onehot.astype(F32)).astype(BF16)
    grad_two = dot(head_ref[...], grad_logits).astype(BF16).astype(F32)
    head_sum[...] += dot(pair_two, grad_logits, 1, 1)

    grad_delta = (grad_two * live).astype(BF16)
    back_two = backward(
        grad_delta,
        normed_two,
        scaling_two,
        gains_ref[:, 1:2],
        second_half,
        second_out_ref,
        act_two,
        slope_two,
        both_two,
    )
    in_sum[...] += dot(inputs_two, both_two[...], 1, 1)
    out_sum[...] += dot(grad_delta, hidden_two[...], 1, 1)

    grad_one = (grad_two + back_two).astype(BF16)
    back_one = backward(
        grad_one,
        normed_one,
        scaling_one,
        gains_ref[:, 0:1],
        first_half,
        first_out_ref,
        act_one,
        slope_one,
        None,
    )
    grad_zero = jnp.transpose(grad_one.astype(F32) + back_one).reshape(block_rows, cols, width)
    pair_grad_ref[...] = grad_zero.astype(BF16)
    left_grad_ref[...] = jnp.sum(grad_zero, axis=1)
    right_grad_ref[...] += jnp.sum(grad_zero, axis=0)

    @pl.when(step == pl.num_programs(0) - 1)
    def _():
        scale = 1.0 / tokens
        row = 0
        for j in range(0, 2 * hid, width):
            factor = scale * 0.5 if j < hid else scale
            weights_ref[row : row + width, :] = (in_sum[:, j : j + width] * factor).astype(BF16)
            row += width
        for j in range(0, hid, width):
            part = jnp.transpose(out_sum[:, j : j + width])
            weights_ref[row : row + width, :] = (part * scale).astype(BF16)
            row += width
        half = width // 2
        packed = jnp.concatenate([head_sum[:half, :], head_sum[half:, :]], axis=1) * scale
        weights_ref[row : row + half, :] = packed.astype(BF16)
        row += half
        if row < weights_ref.shape[0]:
            rest = (weights_ref.shape[0] - row, width)
            weights_ref[row:, :] = jnp.zeros(rest, BF16)


def pair_grid(
    counts,
    order,
    pair_in,
    left_part,
    right_part,
    pae_bins,
    perm_rows,
    perm_cols,
    gain_first,
    first_in,
    first_out,
    gain_second,
    second_in,
    second_out,
    head_weight,
    tokens,
    weight_rows,
):
    rows, cols, width = pair_in.shape
    block_rows = min(BLOCK_ROWS, rows)
    pairs = block_rows * cols
    hid = first_out.shape[0]
    bins = head_weight.shape[1]

    def whole(x):
        return pl.BlockSpec(x.shape, lambda i, *_: (0,) * x.ndim)

    def fixed(*shape):
        return pl.BlockSpec(shape, lambda i, *_: (0,) * len(shape))

    small = (
        right_part,
        pae_bins,
        perm_rows,
        perm_cols,
        gain_first,
        first_in,
        first_out,
        gain_second,
        second_in,
        second_out,
        head_weight,
    )
    grid_spec = pltpu.PrefetchScalarGridSpec(
        num_scalar_prefetch=2,
        grid=(rows // block_rows,),
        in_specs=[
            pl.BlockSpec((block_rows, cols, width), lambda i, *_: (i, 0, 0)),
            pl.BlockSpec((block_rows, width), lambda i, *_: (i, 0)),
        ]
        + [whole(x) for x in small],
        out_specs=[
            pl.BlockSpec((block_rows, cols, width), lambda i, *_: (i, 0, 0)),
            pl.BlockSpec((block_rows, width), lambda i, *_: (i, 0)),
            fixed(cols, width),
            fixed(weight_rows, width),
        ],
        scratch_shapes=[
            pltpu.SMEM((rows * cols // TILE,), F32),
            pltpu.VMEM((rows * cols // LANES, LANES), F32),
            pltpu.VMEM((rows, cols), F32),
            pltpu.VMEM((width, 2), F32),
            pltpu.VMEM((width, 2 * hid), BF16),
            pltpu.VMEM((width, 2 * hid), BF16),
            pltpu.VMEM((2 * hid, width), BF16),
            pltpu.VMEM((2 * hid, width), BF16),
            pltpu.VMEM((width, hid), BF16),
            pltpu.VMEM((width, hid), BF16),
            pltpu.VMEM((bins, width), BF16),
            pltpu.VMEM((hid, pairs), BF16),
            pltpu.VMEM((hid, pairs), BF16),
            pltpu.VMEM((hid, pairs), BF16),
            pltpu.VMEM((hid, pairs), BF16),
            pltpu.VMEM((hid, pairs), BF16),
            pltpu.VMEM((2 * hid, pairs), BF16),
            pltpu.VMEM((width, 2 * hid), F32),
            pltpu.VMEM((width, hid), F32),
            pltpu.VMEM((width, bins), F32),
        ],
    )
    macs = rows * cols * width * (16 * hid + 3 * bins)
    return pl.pallas_call(
        functools.partial(pair_kernel, tokens),
        grid_spec=grid_spec,
        out_shape=[
            jax.ShapeDtypeStruct((rows, cols, width), BF16),
            jax.ShapeDtypeStruct((rows, width), F32),
            jax.ShapeDtypeStruct((cols, width), F32),
            jax.ShapeDtypeStruct((weight_rows, width), BF16),
        ],
        compiler_params=pltpu.CompilerParams(
            vmem_limit_bytes=56 << 20, dimension_semantics=("arbitrary",)
        ),
        cost_estimate=pl.CostEstimate(
            flops=2 * macs,
            bytes_accessed=4 * rows * cols * width,
            transcendentals=2 * rows * cols * hid,
        ),
    )(counts, order, pair_in, left_part, *small)


def swap(x, axis, size, mask):
    return lax.ppermute(x, axis, [(i, i ^ mask) for i in range(size)])


def tree_sum(parts):
    parts = [p.astype(F32) for p in parts]
    while len(parts) > 1:
        parts = [parts[k] + parts[k + 1] for k in range(0, len(parts), 2)]
    return parts[0]


def in_order(parts, index):
    parts = list(parts)
    bit = 1
    while bit < len(parts):
        parts = [
            jnp.where((index & bit) != 0, parts[k ^ bit], parts[k]) for k in range(len(parts))
        ]
        bit *= 2
    return jnp.stack(parts)


def local(
    n_row,
    n_col,
    singles,
    pair_in,
    proj_weight,
    gain_first,
    first_in,
    first_out,
    gain_second,
    second_in,
    second_out,
    head_weight,
    pae_bins,
    chain_perm,
    resolved_counts,
    tile_order,
):
    rows, cols, width = pair_in.shape
    tokens = chain_perm.shape[0]
    hid = first_out.shape[0]
    bins = head_weight.shape[1]
    row_index = lax.axis_index("row")
    col_index = lax.axis_index("col")
    ratio = rows // cols

    joined = jnp.concatenate([singles.T, proj_weight], axis=1)
    joined = lax.all_gather(joined, "col", axis=0, tiled=True)
    projected = dot(joined[:, :rows], joined[:, rows:], 0, 0)
    left_part = projected[:, :width]
    own_half = lax.dynamic_slice_in_dim(
        projected[:, width:], (col_index % ratio) * cols, cols, 0
    ).astype(BF16)
    right_part = lax.ppermute(
        own_half,
        ("row", "col"),
        [
            ((c // ratio) * n_col + z * ratio + c % ratio, z * n_col + c)
            for z in range(n_row)
            for c in range(n_col)
        ],
    )

    used_rows = 3 * hid + width // 2
    share = -(-used_rows // (n_col * 16)) * 16
    pair_grad, left_grad, right_grad, weights = pair_grid(
        resolved_counts,
        tile_order,
        pair_in,
        left_part,
        right_part,
        pae_bins,
        chain_perm.reshape(n_row, rows),
        chain_perm.reshape(n_col, cols),
        gain_first.reshape(1, width),
        first_in,
        first_out,
        gain_second.reshape(1, width),
        second_in,
        second_out,
        head_weight,
        tokens,
        share * n_col,
    )

    right_sent = right_grad.astype(BF16)
    right_parts = [right_sent] + [swap(right_sent, "row", n_row, k) for k in range(1, n_row)]
    right_total = tree_sum(right_parts).astype(BF16)
    spread = [
        lax.ppermute(
            right_total,
            ("row", "col"),
            [
                (z * n_col + c, (c // ratio) * n_col + z * ratio + (p ^ (c % ratio)))
                for z in range(n_row)
                for c in range(n_col)
            ],
        )
        for p in range(ratio)
    ]
    right_tokens = in_order(spread, col_index % ratio).reshape(rows, width)

    left_share = left_grad.astype(BF16).reshape(n_col, rows // n_col, width)
    buffer = jnp.concatenate([weights.reshape(n_col, share, width), left_share], axis=1)
    depth = buffer.shape[1]
    chips = n_col // 2
    chip, core = col_index // 2, col_index % 2
    buffer = buffer.reshape(chips, 2, depth, width)
    kept = lax.dynamic_index_in_dim(buffer, core, 1, keepdims=False)
    sent = lax.dynamic_index_in_dim(buffer, 1 - core, 1, keepdims=False)
    buffer = tree_sum([kept, swap(sent, "col", n_col, 1)]).astype(BF16)
    parts = [lax.dynamic_index_in_dim(buffer, chip, 0, keepdims=False)]
    for k in range(1, chips):
        sent = lax.dynamic_index_in_dim(buffer, chip ^ k, 0, keepdims=False)
        parts.append(swap(sent, "col", n_col, 2 * k))
    buffer = tree_sum(parts).astype(BF16)
    own = buffer[:share]
    own = tree_sum([own] + [swap(own, "row", n_row, k) for k in range(1, n_row)]).astype(BF16)
    buffer = jnp.concatenate([own, buffer[share:]], axis=0)
    buffer = in_order(
        [buffer] + [swap(buffer, "col", n_col, 2 * k) for k in range(1, chips)], chip
    )
    buffer = in_order([buffer, swap(buffer, "col", n_col, 1)], core)
    buffer = buffer.transpose(1, 0, 2, 3).reshape(n_col, depth, width)
    left_tokens = buffer[:, share:].reshape(rows, width)
    weights = buffer[:, :share].reshape(share * n_col, width).astype(F32)

    token_rows = jnp.concatenate([left_tokens, right_tokens], axis=1)
    single_grad = dot(token_rows, proj_weight, 1, 1)
    in_grad = weights[: 2 * hid].reshape(2 * hid // width, width, width)
    in_grad = in_grad.transpose(1, 0, 2).reshape(width, 2 * hid)
    out_grad = weights[2 * hid : 3 * hid]
    head_rows = weights[3 * hid : 3 * hid + width // 2]
    head_grad = jnp.concatenate([head_rows[:, :bins], head_rows[:, bins:]], axis=0)
    return pair_grad, single_grad, in_grad, out_grad, head_grad


def solution(mesh):
    in_specs = (
        P("row", "col"),
        P("row", "col", None),
        P("col", None),
        P(),
        P(),
        P(),
        P(),
        P(),
        P(),
        P(),
        P("row", "col"),
        P(),
        P("row", None),
        P("row", "col"),
    )
    out_specs = (P("row", "col", None), P("row", "col"), P(), P(), P())
    return jax.shard_map(
        functools.partial(local, mesh.shape["row"], mesh.shape["col"]),
        mesh=mesh,
        in_specs=in_specs,
        out_specs=out_specs,
        check_vma=False,
    )
```

```python
import functools

import jax
import jax.numpy as jnp
from jax import lax
from jax.experimental import pallas as pl
from jax.experimental.pallas import tpu as pltpu
from jax.sharding import PartitionSpec as P

TILE = 32
LANES = 128
BLOCK_ROWS = 32
CHUNK = 256
VMEM_LIMIT = 48 << 20
F32 = jnp.float32
BF16 = jnp.bfloat16


def dot(left_op, right_op, left_dim=1, right_dim=0):
    return lax.dot_general(
        left_op,
        right_op,
        (((left_dim,), (right_dim,)), ((), ())),
        preferred_element_type=F32,
    )


def norm(field):
    centred = field - jnp.mean(field, axis=0, keepdims=True)
    scaling = lax.rsqrt(jnp.mean(centred * centred, axis=0, keepdims=True) + 1e-05)
    return centred * scaling, scaling


def forward(inputs, in_turned, out_turned, act_ref, slope_ref, hidden_ref):
    hid = out_turned.shape[1]
    result = None
    for j in range(0, hid, CHUNK):
        half_gate = dot(in_turned[j : j + CHUNK, :], inputs).astype(BF16)
        up = dot(in_turned[hid + j : hid + j + CHUNK, :], inputs).astype(BF16)
        twice_sig = 1.0 + jnp.tanh(half_gate)
        act = half_gate * twice_sig
        hidden = act * up
        act_ref[j : j + CHUNK, :] = act
        slope_ref[j : j + CHUNK, :] = up * (twice_sig + act * (2.0 - twice_sig))
        if hidden_ref is not None:
            hidden_ref[j : j + CHUNK, :] = hidden
        part = dot(out_turned[:, j : j + CHUNK], hidden)
        result = part if result is None else result + part
    return result


def backward(grad_out, normed, scaling, gain, w_in, w_out, act_ref, slope_ref, both_ref):
    hid = w_out.shape[0]
    grad_normed = None
    for j in range(0, hid, CHUNK):
        grad_hidden = dot(w_out[j : j + CHUNK, :], grad_out).astype(BF16)
        grad_gate = grad_hidden * slope_ref[j : j + CHUNK, :]
        grad_up = grad_hidden * act_ref[j : j + CHUNK, :]
        if both_ref is not None:
            both_ref[j : j + CHUNK, :] = grad_gate
            both_ref[hid + j : hid + j + CHUNK, :] = grad_up
        part = dot(w_in[:, j : j + CHUNK], grad_gate)
        part = part + dot(w_in[:, hid + j : hid + j + CHUNK], grad_up)
        grad_normed = part if grad_normed is None else grad_normed + part
    grad_normed = grad_normed * gain
    mean = jnp.mean(grad_normed, axis=0, keepdims=True)
    slant = jnp.mean(grad_normed * normed, axis=0, keepdims=True)
    return scaling * (grad_normed - mean - normed * slant)


def turned(x):
    return jnp.transpose(x.astype(F32)).astype(x.dtype)


def prepare_kernel(
    counts_ref,
    order_ref,
    bins_ref,
    perm_ref,
    gain_first_ref,
    first_in_ref,
    first_out_ref,
    gain_second_ref,
    second_in_ref,
    second_out_ref,
    head_ref,
    first_half,
    first_in_turned,
    first_out_turned,
    second_half,
    second_in_turned,
    second_out_turned,
    head_turned,
    gains_ref,
    live_ref,
    target_ref,
    tile_ref,
    rows_ref,
):
    cols, rows = bins_ref.shape
    hid = first_out_ref.shape[0]
    group = LANES // cols
    row_index, col_index = lax.axis_index("row"), lax.axis_index("col")
    for half, half_turned, whole in (
        (first_half, first_in_turned, first_in_ref),
        (second_half, second_in_turned, second_in_ref),
    ):
        half[:, :hid] = whole[:, :hid] * jnp.asarray(0.5, BF16)
        half[:, hid:] = whole[:, hid:]
        half_turned[...] = turned(half[...])
    first_out_turned[...] = turned(first_out_ref[...])
    second_out_turned[...] = turned(second_out_ref[...])
    head_turned[...] = turned(head_ref[...])
    gains_ref[:, 0:1] = jnp.transpose(gain_first_ref[...])
    gains_ref[:, 1:2] = jnp.transpose(gain_second_ref[...])

    count = counts_ref[0, col_index]

    def place(t, carry):
        tile_ref[order_ref[0, t]] = jnp.where(t < count, 1.0, 0.0).astype(F32)
        return carry

    lax.fori_loop(0, order_ref.shape[1], place, 0, unroll=8)
    lane_tile = lax.broadcasted_iota(jnp.int32, (1, LANES), 1) // TILE
    tiles = LANES // TILE
    for k in range(live_ref.shape[0]):
        part = jnp.full((1, LANES), tile_ref[k * tiles], F32)
        for t in range(1, tiles):
            part = jnp.where(lane_tile == t, tile_ref[k * tiles + t], part)
        live_ref[k : k + 1, :] = part

    perm_rows = perm_ref[pl.ds(row_index, 1), :] - row_index * rows
    perm_line = perm_ref[pl.ds(col_index // (rows // cols), 1), :] - col_index * cols
    perm_cols = perm_line[:, :cols]
    for k in range(1, rows // cols):
        other = perm_line[:, k * cols : (k + 1) * cols]
        perm_cols = jnp.where(lax.rem(col_index, rows // cols) == k, other, perm_cols)
    pick_rows = (lax.broadcasted_iota(jnp.int32, (rows, rows), 0) == perm_rows).astype(BF16)
    pick_cols = (lax.broadcasted_iota(jnp.int32, (cols, cols), 0) == perm_cols).astype(BF16)
    bins = bins_ref[...].astype(F32).astype(BF16)
    moved = dot(pick_rows, bins, 0, 1).astype(BF16)
    rows_ref[...] = dot(moved, pick_cols)
    target_ref[...] = jnp.concatenate(
        [rows_ref[pl.ds(k, rows // group, stride=group), :] for k in range(group)], axis=1
    )


def prepare(
    counts,
    order,
    bins,
    perm,
    gain_first,
    first_in,
    first_out,
    gain_second,
    second_in,
    second_out,
    head,
):
    cols, rows = bins.shape
    width, double = first_in.shape
    hid = first_out.shape[0]
    lines = rows * cols // LANES
    shapes = [
        ((width, double), BF16),
        ((double, width), BF16),
        ((width, hid), BF16),
        ((width, double), BF16),
        ((double, width), BF16),
        ((width, hid), BF16),
        ((width, head.shape[0]), BF16),
        ((width, 2), F32),
        ((lines, LANES), F32),
        ((lines, LANES), F32),
    ]
    smem, vmem = pl.BlockSpec(memory_space=pltpu.SMEM), pl.BlockSpec(memory_space=pltpu.VMEM)
    return pl.pallas_call(
        prepare_kernel,
        in_specs=[smem, smem] + [vmem] * 9,
        out_specs=[vmem] * len(shapes),
        out_shape=[jax.ShapeDtypeStruct(shape, dtype) for shape, dtype in shapes],
        scratch_shapes=[
            pltpu.SMEM((rows * cols // TILE,), F32),
            pltpu.VMEM((rows, cols), F32),
        ],
        compiler_params=pltpu.CompilerParams(vmem_limit_bytes=16 << 20),
        cost_estimate=pl.CostEstimate(
            flops=1 << 30, bytes_accessed=4 << 20, transcendentals=0
        ),
    )(
        counts,
        order,
        bins,
        perm,
        gain_first,
        first_in,
        first_out,
        gain_second,
        second_in,
        second_out,
        head,
    )


def pair_kernel(
    tokens,
    pair_ref,
    left_ref,
    right_ref,
    first_out_ref,
    second_out_ref,
    head_turned,
    first_half,
    first_in_turned,
    first_out_turned,
    second_half,
    second_in_turned,
    second_out_turned,
    head_ref,
    gains_ref,
    live_ref,
    target_ref,
    pair_grad_ref,
    buffer_ref,
    right_grad_ref,
    act_one,
    slope_one,
    act_two,
    slope_two,
    hidden_two,
    both_two,
    in_sum,
    out_sum,
    head_sum,
    right_sum,
):
    block_rows, cols, width = pair_ref.shape
    pairs = block_rows * cols
    hid = first_out_ref.shape[0]
    step = pl.program_id(0)
    vectors = pairs // LANES
    blocks, depth, _ = buffer_ref.shape
    own_rows = pl.num_programs(0) * block_rows // blocks
    share = depth - max(own_rows, 16)

    @pl.when(step == 0)
    def _():
        right_sum[...] = jnp.zeros_like(right_sum)
        in_sum[...] = jnp.zeros_like(in_sum)
        out_sum[...] = jnp.zeros_like(out_sum)
        head_sum[...] = jnp.zeros_like(head_sum)
        buffer_ref[...] = jnp.zeros_like(buffer_ref)

    field = pair_ref[...].astype(F32) + left_ref[:, :width][:, None, :]
    field = (field + right_ref[...].astype(F32)[None]).reshape(pairs, width)
    field = jnp.transpose(field)
    normed_one, scaling_one = norm(field)
    inputs_one = (normed_one * gains_ref[:, 0:1]).astype(BF16)
    delta_one = forward(inputs_one, first_in_turned, first_out_turned, act_one, slope_one, None)
    pair_one = (field + delta_one).astype(BF16).astype(F32)

    normed_two, scaling_two = norm(pair_one)
    inputs_two = (normed_two * gains_ref[:, 1:2]).astype(BF16)
    delta_two = forward(
        inputs_two, second_in_turned, second_out_turned, act_two, slope_two, hidden_two
    )
    live = jnp.concatenate(
        [live_ref[pl.ds(step * vectors + k, 1), :] for k in range(vectors)], axis=1
    )
    pair_two = (pair_one + live * delta_two).astype(BF16)

    logits = dot(head_turned[...], pair_two)
    exponent = jnp.exp(logits - jnp.max(logits, axis=0, keepdims=True))
    probability = exponent * (1.0 / jnp.sum(exponent, axis=0, keepdims=True))
    target = jnp.concatenate(
        [target_ref[pl.ds(step * vectors + k, 1), :] for k in range(vectors)], axis=1
    ).astype(jnp.int32)
    onehot = lax.broadcasted_iota(jnp.int32, logits.shape, 0) == target
    grad_logits = (probability - onehot.astype(F32)).astype(BF16)
    grad_two = dot(head_ref[...], grad_logits).astype(BF16).astype(F32)
    head_sum[...] += dot(grad_logits, pair_two, 1, 1)

    grad_delta = (grad_two * live).astype(BF16)
    back_two = backward(
        grad_delta,
        normed_two,
        scaling_two,
        gains_ref[:, 1:2],
        second_half,
        second_out_ref,
        act_two,
        slope_two,
        both_two,
    )
    in_sum[...] += dot(inputs_two, both_two[...], 1, 1)
    out_sum[...] += dot(grad_delta, hidden_two[...], 1, 1)

    grad_one = (grad_two + back_two).astype(BF16)
    back_one = backward(
        grad_one,
        normed_one,
        scaling_one,
        gains_ref[:, 0:1],
        first_half,
        first_out_ref,
        act_one,
        slope_one,
        None,
    )
    grad_zero = jnp.transpose(grad_one.astype(F32) + back_one).reshape(block_rows, cols, width)
    pair_grad_ref[...] = grad_zero.astype(BF16)
    right_sum[...] += jnp.sum(grad_zero, axis=0)
    left_grad = jnp.sum(grad_zero, axis=1).astype(BF16)
    per_step = block_rows // own_rows
    for k in range(per_step):
        part = left_grad[k * own_rows : (k + 1) * own_rows]
        buffer_ref[step * per_step + k, share : share + own_rows, :] = part

    @pl.when(step == pl.num_programs(0) - 1)
    def _():
        scale = 1.0 / tokens
        right_grad_ref[...] = right_sum[...].astype(BF16)
        parts = []
        for j in range(0, 2 * hid, width):
            factor = scale * 0.5 if j < hid else scale
            parts.append((in_sum[:, j : j + width] * factor).astype(BF16))
        for j in range(0, hid, width):
            parts.append((jnp.transpose(out_sum[:, j : j + width]) * scale).astype(BF16))
        parts.append((head_sum[...] * scale).astype(BF16))
        first = 0
        for part in parts:
            for block, offset, start, stop in pieces(first, part.shape[0], share):
                buffer_ref[block, offset : offset + stop - start, :] = part[start:stop]
            first += part.shape[0]


def pieces(first, count, share):
    found, at = [], first
    while at < first + count:
        stop = min(first + count, (at // share + 1) * share)
        found.append((at // share, at % share, at - first, stop - first))
        at = stop
    return found


def unpack_kernel(share, gathered_ref, proj_ref, in_ref, out_ref, head_ref, single_ref):
    width, double = in_ref.shape
    cols = gathered_ref.shape[1] - share
    blocks = gathered_ref.shape[0]
    rows = single_ref.shape[1]
    own_rows = rows // blocks
    cols -= max(own_rows, 16)

    def put(first, count, ref, row, col):
        for block, offset, start, stop in pieces(first, count, share):
            part = gathered_ref[block, offset : offset + stop - start, :].astype(F32)
            ref[row + start : row + stop, col : col + width] = part

    for j in range(0, double, width):
        put(j, width, in_ref, 0, j)
    put(double, out_ref.shape[0], out_ref, 0, 0)
    put(double + out_ref.shape[0], head_ref.shape[0], head_ref, 0, 0)
    at = share + cols
    left = jnp.concatenate(
        [gathered_ref[b, at : at + own_rows, :].astype(F32) for b in range(blocks)], axis=0
    ).astype(BF16)
    ratio = rows // cols
    first = lax.axis_index("row") * ratio
    right = jnp.concatenate(
        [gathered_ref[first + k, share : share + cols, :] for k in range(ratio)], axis=0
    )
    single = dot(proj_ref[:, :width], left, 1, 1)
    single_ref[...] = single + dot(proj_ref[:, width:], right, 1, 1)


def unpack(gathered, proj_weight, hid, bins, rows, share):
    width = gathered.shape[2]
    shapes = [(width, 2 * hid), (hid, width), (bins, width), (proj_weight.shape[0], rows)]
    vmem = pl.BlockSpec(memory_space=pltpu.VMEM)
    return pl.pallas_call(
        functools.partial(unpack_kernel, share),
        in_specs=[vmem, vmem],
        out_specs=[vmem] * 4,
        out_shape=[jax.ShapeDtypeStruct(shape, F32) for shape in shapes],
        compiler_params=pltpu.CompilerParams(vmem_limit_bytes=16 << 20),
    )(gathered, proj_weight)


def pair_grid(
    pair_in,
    projected,
    right_part,
    first_out,
    second_out,
    head_turned,
    prepared,
    tokens,
    n_col,
    share,
):
    rows, cols, width = pair_in.shape
    block_rows = min(BLOCK_ROWS, rows)
    pairs = block_rows * cols
    hid = first_out.shape[0]
    bins = head_turned.shape[0]
    depth = share + max(rows // n_col, 16)

    def whole(x):
        return pl.BlockSpec(x.shape, lambda i: (0,) * x.ndim)

    def fixed(*shape):
        return pl.BlockSpec(shape, lambda i: (0,) * len(shape))

    small = (right_part, first_out, second_out, head_turned, *prepared)
    macs = rows * cols * width * (16 * hid + 3 * bins)
    return pl.pallas_call(
        functools.partial(pair_kernel, tokens),
        grid=(rows // block_rows,),
        in_specs=[
            pl.BlockSpec((block_rows, cols, width), lambda i: (i, 0, 0)),
            pl.BlockSpec((block_rows, projected.shape[1]), lambda i: (i, 0)),
        ]
        + [whole(x) for x in small],
        out_specs=[
            pl.BlockSpec((block_rows, cols, width), lambda i: (i, 0, 0)),
            fixed(n_col, depth, width),
            fixed(cols, width),
        ],
        scratch_shapes=[
            pltpu.VMEM((hid, pairs), BF16),
            pltpu.VMEM((hid, pairs), BF16),
            pltpu.VMEM((hid, pairs), BF16),
            pltpu.VMEM((hid, pairs), BF16),
            pltpu.VMEM((hid, pairs), BF16),
            pltpu.VMEM((2 * hid, pairs), BF16),
            pltpu.VMEM((width, 2 * hid), F32),
            pltpu.VMEM((width, hid), F32),
            pltpu.VMEM((bins, width), F32),
            pltpu.VMEM((cols, width), F32),
        ],
        out_shape=[
            jax.ShapeDtypeStruct((rows, cols, width), BF16),
            jax.ShapeDtypeStruct((n_col, depth, width), BF16),
            jax.ShapeDtypeStruct((cols, width), BF16),
        ],
        compiler_params=pltpu.CompilerParams(
            vmem_limit_bytes=VMEM_LIMIT, dimension_semantics=("arbitrary",)
        ),
        cost_estimate=pl.CostEstimate(
            flops=2 * macs,
            bytes_accessed=4 * rows * cols * width,
            transcendentals=2 * rows * cols * hid,
        ),
    )(pair_in, projected, *small)


def swap(x, axis, size, mask):
    return lax.ppermute(x, axis, [(i, i ^ mask) for i in range(size)])


def tree_sum(parts):
    parts = [p.astype(F32) for p in parts]
    while len(parts) > 1:
        parts = [parts[k] + parts[k + 1] for k in range(0, len(parts), 2)]
    return parts[0]


def local(
    n_row,
    n_col,
    singles,
    pair_in,
    proj_weight,
    gain_first,
    first_in,
    first_out,
    gain_second,
    second_in,
    second_out,
    head_weight,
    pae_bins,
    chain_perm,
    resolved_counts,
    tile_order,
):
    rows, cols, width = pair_in.shape
    tokens = chain_perm.shape[0]
    hid = first_out.shape[0]
    bins = head_weight.shape[1]
    col_index = lax.axis_index("col")
    ratio = rows // cols

    joined = jnp.concatenate([singles.T, proj_weight], axis=1)
    joined = lax.all_gather(joined, "col", axis=0, tiled=True)
    projected = dot(joined[:, :rows], joined[:, rows:], 0, 0)
    own_half = lax.dynamic_slice_in_dim(
        projected[:, width:], (col_index % ratio) * cols, cols, 0
    ).astype(BF16)
    right_part = lax.ppermute(
        own_half,
        ("row", "col"),
        [
            ((c // ratio) * n_col + z * ratio + c % ratio, z * n_col + c)
            for z in range(n_row)
            for c in range(n_col)
        ],
    )
    head_turned = head_weight.T
    prepared = prepare(
        resolved_counts,
        tile_order,
        pae_bins.T,
        chain_perm.reshape(n_row, rows),
        gain_first.reshape(1, width),
        first_in,
        first_out,
        gain_second.reshape(1, width),
        second_in,
        second_out,
        head_turned,
    )

    share = -(-(3 * hid + bins) // (n_col * 16)) * 16
    pair_grad, buffer, right_grad = pair_grid(
        pair_in,
        projected,
        right_part,
        first_out,
        second_out,
        head_turned,
        prepared,
        tokens,
        n_col,
        share,
    )

    buffer = lax.all_to_all(buffer, "col", 0, 0, tiled=True)
    buffer = tree_sum([buffer[k] for k in range(n_col)]).astype(BF16)
    own = jnp.concatenate([buffer[:share], right_grad], axis=0)
    own = tree_sum([own] + [swap(own, "row", n_row, k) for k in range(1, n_row)]).astype(BF16)
    own = jnp.concatenate([own, buffer[share:]], axis=0)
    gathered = lax.all_gather(own, "col", axis=0)
    in_grad, out_grad, head_grad, single_grad = unpack(
        gathered, proj_weight, hid, bins, rows, share
    )
    return pair_grad, single_grad.T, in_grad, out_grad, head_grad.T


def solution(mesh):
    in_specs = (
        P("row", "col"),
        P("row", "col", None),
        P("col", None),
        P(),
        P(),
        P(),
        P(),
        P(),
        P(),
        P(),
        P("row", "col"),
        P(),
        P("row", None),
        P("row", "col"),
    )
    out_specs = (P("row", "col", None), P("row", "col"), P(), P(), P())
    return jax.shard_map(
        functools.partial(local, mesh.shape["row"], mesh.shape["col"]),
        mesh=mesh,
        in_specs=in_specs,
        out_specs=out_specs,
        check_vma=False,
    )
```

```python
import functools

import jax
import jax.numpy as jnp
from jax import lax
from jax.experimental import pallas as pl
from jax.experimental.pallas import tpu as pltpu
from jax.sharding import PartitionSpec as P

TILE = 32
LANES = 128
BLOCK_ROWS = 32
CHUNK = 256
VMEM_LIMIT = 61 << 20
PARTS = 2
AHEAD = 2
F32 = jnp.float32
BF16 = jnp.bfloat16


def dot(left_op, right_op, left_dim=1, right_dim=0):
    return lax.dot_general(
        left_op,
        right_op,
        (((left_dim,), (right_dim,)), ((), ())),
        preferred_element_type=F32,
    )


def norm(field):
    centred = field - jnp.mean(field, axis=0, keepdims=True)
    scaling = lax.rsqrt(jnp.mean(centred * centred, axis=0, keepdims=True) + 1e-05)
    return centred * scaling, scaling


def forward(inputs, in_turned, out_turned, act_ref, slope_ref, hidden_ref, lanes):
    hid = out_turned.shape[1]
    result = None
    for j in range(0, hid, CHUNK):
        half_gate = dot(in_turned[j : j + CHUNK, :], inputs).astype(BF16)
        up = dot(in_turned[hid + j : hid + j + CHUNK, :], inputs).astype(BF16)
        yield
        twice_sig = 1.0 + jnp.tanh(half_gate)
        act = half_gate * twice_sig
        hidden = act * up
        act_ref[j : j + CHUNK, lanes] = act
        slope_ref[j : j + CHUNK, lanes] = up * (twice_sig + act * (2.0 - twice_sig))
        if hidden_ref is not None:
            hidden_ref[j : j + CHUNK, lanes] = hidden
        yield
        part = dot(out_turned[:, j : j + CHUNK], hidden)
        result = part if result is None else result + part
    return result


def backward(grad_out, normed, scaling, gain, w_in, w_out, act_ref, slope_ref, both_ref, lanes):
    hid = w_out.shape[0]
    grad_normed = None
    for j in range(0, hid, CHUNK):
        grad_hidden = dot(w_out[j : j + CHUNK, :], grad_out).astype(BF16)
        yield
        grad_gate = grad_hidden * slope_ref[j : j + CHUNK, lanes]
        grad_up = grad_hidden * act_ref[j : j + CHUNK, lanes]
        if both_ref is not None:
            both_ref[j : j + CHUNK, lanes] = grad_gate
            both_ref[hid + j : hid + j + CHUNK, lanes] = grad_up
        yield
        part = dot(w_in[:, j : j + CHUNK], grad_gate)
        part = part + dot(w_in[:, hid + j : hid + j + CHUNK], grad_up)
        grad_normed = part if grad_normed is None else grad_normed + part
    grad_normed = grad_normed * gain
    mean = jnp.mean(grad_normed, axis=0, keepdims=True)
    slant = jnp.mean(grad_normed * normed, axis=0, keepdims=True)
    return scaling * (grad_normed - mean - normed * slant)


def turned(x):
    return jnp.transpose(x.astype(F32)).astype(x.dtype)


def prepare_kernel(
    counts_ref,
    order_ref,
    bins_ref,
    perm_ref,
    gain_first_ref,
    first_in_ref,
    first_out_ref,
    gain_second_ref,
    second_in_ref,
    second_out_ref,
    head_ref,
    first_half,
    first_in_turned,
    first_out_turned,
    second_half,
    second_in_turned,
    second_out_turned,
    head_turned,
    gains_ref,
    live_ref,
    target_ref,
    tile_ref,
    rows_ref,
):
    cols, rows = bins_ref.shape
    hid = first_out_ref.shape[0]
    group = LANES // cols
    row_index, col_index = lax.axis_index("row"), lax.axis_index("col")
    for half, half_turned, whole in (
        (first_half, first_in_turned, first_in_ref),
        (second_half, second_in_turned, second_in_ref),
    ):
        half[:, :hid] = whole[:, :hid] * jnp.asarray(0.5, BF16)
        half[:, hid:] = whole[:, hid:]
        half_turned[...] = turned(half[...])
    first_out_turned[...] = turned(first_out_ref[...])
    second_out_turned[...] = turned(second_out_ref[...])
    head_turned[...] = turned(head_ref[...])
    gains_ref[:, 0:1] = jnp.transpose(gain_first_ref[...])
    gains_ref[:, 1:2] = jnp.transpose(gain_second_ref[...])

    count = counts_ref[0, col_index]

    def place(t, carry):
        tile_ref[order_ref[0, t]] = jnp.where(t < count, 1.0, 0.0).astype(F32)
        return carry

    lax.fori_loop(0, order_ref.shape[1], place, 0, unroll=8)
    lane_tile = lax.broadcasted_iota(jnp.int32, (1, LANES), 1) // TILE
    tiles = LANES // TILE
    for k in range(live_ref.shape[0]):
        part = jnp.full((1, LANES), tile_ref[k * tiles], F32)
        for t in range(1, tiles):
            part = jnp.where(lane_tile == t, tile_ref[k * tiles + t], part)
        live_ref[k : k + 1, :] = part

    perm_rows = perm_ref[pl.ds(row_index, 1), :] - row_index * rows
    perm_line = perm_ref[pl.ds(col_index // (rows // cols), 1), :] - col_index * cols
    perm_cols = perm_line[:, :cols]
    for k in range(1, rows // cols):
        other = perm_line[:, k * cols : (k + 1) * cols]
        perm_cols = jnp.where(lax.rem(col_index, rows // cols) == k, other, perm_cols)
    pick_rows = (lax.broadcasted_iota(jnp.int32, (rows, rows), 0) == perm_rows).astype(BF16)
    pick_cols = (lax.broadcasted_iota(jnp.int32, (cols, cols), 0) == perm_cols).astype(BF16)
    bins = bins_ref[...].astype(F32).astype(BF16)
    moved = dot(pick_rows, bins, 0, 1).astype(BF16)
    rows_ref[...] = dot(moved, pick_cols)
    target_ref[...] = jnp.concatenate(
        [rows_ref[pl.ds(k, rows // group, stride=group), :] for k in range(group)], axis=1
    )


def prepare(
    counts,
    order,
    bins,
    perm,
    gain_first,
    first_in,
    first_out,
    gain_second,
    second_in,
    second_out,
    head,
):
    cols, rows = bins.shape
    width, double = first_in.shape
    hid = first_out.shape[0]
    lines = rows * cols // LANES
    shapes = [
        ((width, double), BF16),
        ((double, width), BF16),
        ((width, hid), BF16),
        ((width, double), BF16),
        ((double, width), BF16),
        ((width, hid), BF16),
        ((width, head.shape[0]), BF16),
        ((width, 2), F32),
        ((lines, LANES), F32),
        ((lines, LANES), F32),
    ]
    small = (
        bins,
        perm,
        gain_first,
        first_in,
        first_out,
        gain_second,
        second_in,
        second_out,
        head,
    )
    return pl.pallas_call(
        prepare_kernel,
        grid_spec=pltpu.PrefetchScalarGridSpec(
            num_scalar_prefetch=2,
            grid=(1,),
            in_specs=[pl.BlockSpec(x.shape, lambda i, *_: (0, 0)) for x in small],
            out_specs=[pl.BlockSpec(shape, lambda i, *_: (0, 0)) for shape, _ in shapes],
            scratch_shapes=[
                pltpu.SMEM((rows * cols // TILE,), F32),
                pltpu.VMEM((rows, cols), F32),
            ],
        ),
        out_shape=[jax.ShapeDtypeStruct(shape, dtype) for shape, dtype in shapes],
        compiler_params=pltpu.CompilerParams(vmem_limit_bytes=VMEM_LIMIT),
        cost_estimate=pl.CostEstimate(
            flops=1 << 30, bytes_accessed=4 << 20, transcendentals=0
        ),
    )(counts, order, *small)


def pair_kernel(
    tokens,
    pair_ref,
    left_ref,
    right_ref,
    first_out_ref,
    second_out_ref,
    head_turned,
    first_half,
    first_in_turned,
    first_out_turned,
    second_half,
    second_in_turned,
    second_out_turned,
    head_ref,
    gains_ref,
    live_ref,
    target_ref,
    pair_grad_ref,
    buffer_ref,
    right_grad_ref,
    act_one,
    slope_one,
    act_two,
    slope_two,
    hidden_two,
    both_two,
    in_sum,
    out_sum,
    head_sum,
    right_sum,
):
    block_rows, cols, width = pair_ref.shape
    pairs = block_rows * cols
    hid = first_out_ref.shape[0]
    step = pl.program_id(0)
    vectors = pairs // LANES
    blocks, depth, _ = buffer_ref.shape
    own_rows = pl.num_programs(0) * block_rows // blocks
    share = depth - max(own_rows, 16)

    @pl.when(step == 0)
    def _():
        right_sum[...] = jnp.zeros_like(right_sum)
        in_sum[...] = jnp.zeros_like(in_sum)
        out_sum[...] = jnp.zeros_like(out_sum)
        head_sum[...] = jnp.zeros_like(head_sum)
        buffer_ref[...] = jnp.zeros_like(buffer_ref)

    def flow(part_index):
        part_pairs = pairs // PARTS
        part_vectors = vectors // PARTS
        lanes = slice(part_index * part_pairs, (part_index + 1) * part_pairs)
        part_rows = slice(
            part_index * (block_rows // PARTS), (part_index + 1) * (block_rows // PARTS)
        )
        field = pair_ref[part_rows].astype(F32) + left_ref[part_rows, :width][:, None, :]
        field = (field + right_ref[...].astype(F32)[None]).reshape(part_pairs, width)
        field = jnp.transpose(field)
        yield
        normed_one, scaling_one = norm(field)
        inputs_one = (normed_one * gains_ref[:, 0:1]).astype(BF16)
        yield
        delta_one = yield from forward(
            inputs_one, first_in_turned, first_out_turned, act_one, slope_one, None, lanes
        )
        yield
        pair_one = (field + delta_one).astype(BF16).astype(F32)

        normed_two, scaling_two = norm(pair_one)
        inputs_two = (normed_two * gains_ref[:, 1:2]).astype(BF16)
        yield
        delta_two = yield from forward(
            inputs_two, second_in_turned, second_out_turned, act_two, slope_two, hidden_two, lanes
        )
        yield
        line = step * vectors + part_index * part_vectors
        live = jnp.concatenate(
            [live_ref[pl.ds(line + k, 1), :] for k in range(part_vectors)], axis=1
        )
        pair_two = (pair_one + live * delta_two).astype(BF16)

        logits = dot(head_turned[...], pair_two)
        yield
        exponent = jnp.exp(logits - jnp.max(logits, axis=0, keepdims=True))
        probability = exponent * (1.0 / jnp.sum(exponent, axis=0, keepdims=True))
        target = jnp.concatenate(
            [target_ref[pl.ds(line + k, 1), :] for k in range(part_vectors)], axis=1
        ).astype(jnp.int32)
        onehot = lax.broadcasted_iota(jnp.int32, logits.shape, 0) == target
        grad_logits = (probability - onehot.astype(F32)).astype(BF16)
        yield
        grad_two = dot(head_ref[...], grad_logits).astype(BF16).astype(F32)
        head_sum[...] += dot(grad_logits, pair_two, 1, 1)

        grad_delta = (grad_two * live).astype(BF16)
        yield
        back_two = yield from backward(
            grad_delta,
            normed_two,
            scaling_two,
            gains_ref[:, 1:2],
            second_half,
            second_out_ref,
            act_two,
            slope_two,
            both_two,
            lanes,
        )
        in_sum[...] += dot(inputs_two, both_two[:, lanes], 1, 1)
        out_sum[...] += dot(grad_delta, hidden_two[:, lanes], 1, 1)
        yield

        grad_one = (grad_two + back_two).astype(BF16)
        back_one = yield from backward(
            grad_one,
            normed_one,
            scaling_one,
            gains_ref[:, 0:1],
            first_half,
            first_out_ref,
            act_one,
            slope_one,
            None,
            lanes,
        )
        yield
        grad_zero = jnp.transpose(grad_one.astype(F32) + back_one).reshape(-1, cols, width)
        pair_grad_ref[part_rows] = grad_zero.astype(BF16)
        right_sum[...] += jnp.sum(grad_zero, axis=0)
        left_grad = jnp.sum(grad_zero, axis=1).astype(BF16)
        per_part = block_rows // PARTS // own_rows
        per_step = block_rows // own_rows
        for k in range(per_part):
            part = left_grad[k * own_rows : (k + 1) * own_rows]
            buffer_ref[step * per_step + part_index * per_part + k, share : share + own_rows, :] = part

    flows = [flow(k) for k in range(PARTS)]
    for k, each in enumerate(flows):
        for _ in range((PARTS - 1 - k) * AHEAD):
            next(each)
    while flows:
        for each in list(flows):
            if next(each, flows) is flows:
                flows.remove(each)

    @pl.when(step == pl.num_programs(0) - 1)
    def _():
        scale = 1.0 / tokens
        right_grad_ref[...] = right_sum[...].astype(BF16)
        parts = []
        for j in range(0, 2 * hid, width):
            factor = scale * 0.5 if j < hid else scale
            parts.append((in_sum[:, j : j + width] * factor).astype(BF16))
        for j in range(0, hid, width):
            parts.append((jnp.transpose(out_sum[:, j : j + width]) * scale).astype(BF16))
        parts.append((head_sum[...] * scale).astype(BF16))
        first = 0
        for part in parts:
            for block, offset, start, stop in pieces(first, part.shape[0], share):
                buffer_ref[block, offset : offset + stop - start, :] = part[start:stop]
            first += part.shape[0]


def pieces(first, count, share):
    found, at = [], first
    while at < first + count:
        stop = min(first + count, (at // share + 1) * share)
        found.append((at // share, at % share, at - first, stop - first))
        at = stop
    return found


def unpack_kernel(share, gathered_ref, proj_ref, in_ref, out_ref, head_ref, single_ref):
    width, double = in_ref.shape
    cols = gathered_ref.shape[1] - share
    blocks = gathered_ref.shape[0]
    rows = single_ref.shape[1]
    own_rows = rows // blocks
    cols -= max(own_rows, 16)

    def put(first, count, ref, row, col):
        for block, offset, start, stop in pieces(first, count, share):
            part = gathered_ref[block, offset : offset + stop - start, :].astype(F32)
            ref[row + start : row + stop, col : col + width] = part

    for j in range(0, double, width):
        put(j, width, in_ref, 0, j)
    put(double, out_ref.shape[0], out_ref, 0, 0)
    put(double + out_ref.shape[0], head_ref.shape[0], head_ref, 0, 0)
    at = share + cols
    left = jnp.concatenate(
        [gathered_ref[b, at : at + own_rows, :].astype(F32) for b in range(blocks)], axis=0
    ).astype(BF16)
    ratio = rows // cols
    first = lax.axis_index("row") * ratio
    right = jnp.concatenate(
        [gathered_ref[first + k, share : share + cols, :] for k in range(ratio)], axis=0
    )
    single = dot(proj_ref[:, :width], left, 1, 1)
    single_ref[...] = single + dot(proj_ref[:, width:], right, 1, 1)


def unpack(gathered, proj_weight, hid, bins, rows, share):
    width = gathered.shape[2]
    shapes = [(width, 2 * hid), (hid, width), (bins, width), (proj_weight.shape[0], rows)]
    vmem = pl.BlockSpec(memory_space=pltpu.VMEM)
    return pl.pallas_call(
        functools.partial(unpack_kernel, share),
        in_specs=[vmem, vmem],
        out_specs=[vmem] * 4,
        out_shape=[jax.ShapeDtypeStruct(shape, F32) for shape in shapes],
        compiler_params=pltpu.CompilerParams(vmem_limit_bytes=16 << 20),
    )(gathered, proj_weight)


def pair_grid(
    pair_in,
    projected,
    right_part,
    first_out,
    second_out,
    head_turned,
    prepared,
    tokens,
    n_col,
    share,
):
    rows, cols, width = pair_in.shape
    block_rows = min(BLOCK_ROWS, rows)
    pairs = block_rows * cols
    hid = first_out.shape[0]
    bins = head_turned.shape[0]
    depth = share + max(rows // n_col, 16)

    def whole(x):
        return pl.BlockSpec(x.shape, lambda i: (0,) * x.ndim)

    def fixed(*shape):
        return pl.BlockSpec(shape, lambda i: (0,) * len(shape))

    small = (right_part, first_out, second_out, head_turned, *prepared)
    macs = rows * cols * width * (16 * hid + 3 * bins)
    return pl.pallas_call(
        functools.partial(pair_kernel, tokens),
        grid=(rows // block_rows,),
        in_specs=[
            pl.BlockSpec((block_rows, cols, width), lambda i: (i, 0, 0)),
            pl.BlockSpec((block_rows, projected.shape[1]), lambda i: (i, 0)),
        ]
        + [whole(x) for x in small],
        out_specs=[
            pl.BlockSpec((block_rows, cols, width), lambda i: (i, 0, 0)),
            fixed(n_col, depth, width),
            fixed(cols, width),
        ],
        scratch_shapes=[
            pltpu.VMEM((hid, pairs), BF16),
            pltpu.VMEM((hid, pairs), BF16),
            pltpu.VMEM((hid, pairs), BF16),
            pltpu.VMEM((hid, pairs), BF16),
            pltpu.VMEM((hid, pairs), BF16),
            pltpu.VMEM((2 * hid, pairs), BF16),
            pltpu.VMEM((width, 2 * hid), F32),
            pltpu.VMEM((width, hid), F32),
            pltpu.VMEM((bins, width), F32),
            pltpu.VMEM((cols, width), F32),
        ],
        out_shape=[
            jax.ShapeDtypeStruct((rows, cols, width), BF16),
            jax.ShapeDtypeStruct((n_col, depth, width), BF16),
            jax.ShapeDtypeStruct((cols, width), BF16),
        ],
        compiler_params=pltpu.CompilerParams(
            vmem_limit_bytes=VMEM_LIMIT, dimension_semantics=("arbitrary",)
        ),
        cost_estimate=pl.CostEstimate(
            flops=2 * macs,
            bytes_accessed=4 * rows * cols * width,
            transcendentals=2 * rows * cols * hid,
        ),
    )(pair_in, projected, *small)


def swap(x, axis, size, mask):
    return lax.ppermute(x, axis, [(i, i ^ mask) for i in range(size)])


def tree_sum(parts):
    parts = [p.astype(F32) for p in parts]
    while len(parts) > 1:
        parts = [parts[k] + parts[k + 1] for k in range(0, len(parts), 2)]
    return parts[0]


def local(
    n_row,
    n_col,
    singles,
    pair_in,
    proj_weight,
    gain_first,
    first_in,
    first_out,
    gain_second,
    second_in,
    second_out,
    head_weight,
    pae_bins,
    chain_perm,
    resolved_counts,
    tile_order,
):
    rows, cols, width = pair_in.shape
    tokens = chain_perm.shape[0]
    hid = first_out.shape[0]
    bins = head_weight.shape[1]
    col_index = lax.axis_index("col")
    ratio = rows // cols

    joined = jnp.concatenate([singles.T, proj_weight], axis=1)
    joined = lax.all_gather(joined, "col", axis=0, tiled=True)
    projected = dot(joined[:, :rows], joined[:, rows:], 0, 0)
    own_half = lax.dynamic_slice_in_dim(
        projected[:, width:], (col_index % ratio) * cols, cols, 0
    ).astype(BF16)
    right_part = lax.ppermute(
        own_half,
        ("row", "col"),
        [
            ((c // ratio) * n_col + z * ratio + c % ratio, z * n_col + c)
            for z in range(n_row)
            for c in range(n_col)
        ],
    )
    head_turned = head_weight.T
    prepared = prepare(
        resolved_counts,
        tile_order,
        pae_bins.T,
        chain_perm.reshape(n_row, rows),
        gain_first.reshape(1, width),
        first_in,
        first_out,
        gain_second.reshape(1, width),
        second_in,
        second_out,
        head_turned,
    )

    share = -(-(3 * hid + bins) // (n_col * 16)) * 16
    pair_grad, buffer, right_grad = pair_grid(
        pair_in,
        projected,
        right_part,
        first_out,
        second_out,
        head_turned,
        prepared,
        tokens,
        n_col,
        share,
    )

    buffer = lax.all_to_all(buffer, "col", 0, 0, tiled=True)
    buffer = tree_sum([buffer[k] for k in range(n_col)]).astype(BF16)
    own = jnp.concatenate([buffer[:share], right_grad], axis=0)
    own = tree_sum([own] + [swap(own, "row", n_row, k) for k in range(1, n_row)]).astype(BF16)
    own = jnp.concatenate([own, buffer[share:]], axis=0)
    gathered = lax.all_gather(own, "col", axis=0)
    in_grad, out_grad, head_grad, single_grad = unpack(
        gathered, proj_weight, hid, bins, rows, share
    )
    return pair_grad, single_grad.T, in_grad, out_grad, head_grad.T


def solution(mesh):
    in_specs = (
        P("row", "col"),
        P("row", "col", None),
        P("col", None),
        P(),
        P(),
        P(),
        P(),
        P(),
        P(),
        P(),
        P("row", "col"),
        P(),
        P("row", None),
        P("row", "col"),
    )
    out_specs = (P("row", "col", None), P("row", "col"), P(), P(), P())
    return jax.shard_map(
        functools.partial(local, mesh.shape["row"], mesh.shape["col"]),
        mesh=mesh,
        in_specs=in_specs,
        out_specs=out_specs,
        check_vma=False,
    )
```

```python
import functools

import jax
import jax.numpy as jnp
from jax import lax
from jax.experimental import pallas as pl
from jax.experimental.pallas import tpu as pltpu
from jax.sharding import PartitionSpec as P

TILE = 32
LANES = 128
BLOCK_ROWS = 32
CHUNK = 256
VMEM_LIMIT = 61 << 20
PARTS = 2
AHEAD = 2
F32 = jnp.float32
BF16 = jnp.bfloat16


def dot(left_op, right_op, left_dim=1, right_dim=0):
    return lax.dot_general(
        left_op,
        right_op,
        (((left_dim,), (right_dim,)), ((), ())),
        preferred_element_type=F32,
    )


def norm(field):
    centred = field - jnp.mean(field, axis=0, keepdims=True)
    scaling = lax.rsqrt(jnp.mean(centred * centred, axis=0, keepdims=True) + 1e-05)
    return centred * scaling, scaling


def forward(inputs, in_turned, out_turned, act_ref, slope_ref, hidden_ref, lanes):
    hid = out_turned.shape[1]
    result = None
    for j in range(0, hid, CHUNK):
        half_gate = dot(in_turned[j : j + CHUNK, :], inputs).astype(BF16)
        up = dot(in_turned[hid + j : hid + j + CHUNK, :], inputs).astype(BF16)
        yield
        twice_sig = 1.0 + jnp.tanh(half_gate)
        act = half_gate * twice_sig
        hidden = act * up
        act_ref[j : j + CHUNK, lanes] = act
        slope_ref[j : j + CHUNK, lanes] = up * (twice_sig + act * (2.0 - twice_sig))
        if hidden_ref is not None:
            hidden_ref[j : j + CHUNK, lanes] = hidden
        yield
        part = dot(out_turned[:, j : j + CHUNK], hidden)
        result = part if result is None else result + part
    return result


def backward(grad_out, normed, scaling, gain, w_in, w_out, act_ref, slope_ref, both_ref, lanes):
    hid = w_out.shape[0]
    grad_normed = None
    for j in range(0, hid, CHUNK):
        grad_hidden = dot(w_out[j : j + CHUNK, :], grad_out).astype(BF16)
        yield
        grad_gate = grad_hidden * slope_ref[j : j + CHUNK, lanes]
        grad_up = grad_hidden * act_ref[j : j + CHUNK, lanes]
        if both_ref is not None:
            both_ref[j : j + CHUNK, lanes] = grad_gate
            both_ref[hid + j : hid + j + CHUNK, lanes] = grad_up
        yield
        part = dot(w_in[:, j : j + CHUNK], grad_gate)
        part = part + dot(w_in[:, hid + j : hid + j + CHUNK], grad_up)
        grad_normed = part if grad_normed is None else grad_normed + part
    grad_normed = grad_normed * gain
    mean = jnp.mean(grad_normed, axis=0, keepdims=True)
    slant = jnp.mean(grad_normed * normed, axis=0, keepdims=True)
    return scaling * (grad_normed - mean - normed * slant)


def turned(x):
    return jnp.transpose(x.astype(F32)).astype(x.dtype)


def prepare_kernel(
    counts_ref,
    order_ref,
    bins_ref,
    perm_ref,
    gain_first_ref,
    first_in_ref,
    first_out_ref,
    gain_second_ref,
    second_in_ref,
    second_out_ref,
    head_ref,
    first_half,
    first_in_turned,
    first_out_turned,
    second_half,
    second_in_turned,
    second_out_turned,
    head_turned,
    gains_ref,
    live_ref,
    target_ref,
    tile_ref,
    rows_ref,
):
    cols, rows = bins_ref.shape
    hid = first_out_ref.shape[0]
    group = LANES // cols
    row_index, col_index = lax.axis_index("row"), lax.axis_index("col")
    for half, half_turned, whole in (
        (first_half, first_in_turned, first_in_ref),
        (second_half, second_in_turned, second_in_ref),
    ):
        half[:, :hid] = whole[:, :hid] * jnp.asarray(0.5, BF16)
        half[:, hid:] = whole[:, hid:]
        half_turned[...] = turned(half[...])
    first_out_turned[...] = turned(first_out_ref[...])
    second_out_turned[...] = turned(second_out_ref[...])
    head_turned[...] = turned(head_ref[...])
    gains_ref[:, 0:1] = jnp.transpose(gain_first_ref[...])
    gains_ref[:, 1:2] = jnp.transpose(gain_second_ref[...])

    count = counts_ref[0, col_index]

    def place(t, carry):
        tile_ref[order_ref[0, t]] = jnp.where(t < count, 1.0, 0.0).astype(F32)
        return carry

    lax.fori_loop(0, order_ref.shape[1], place, 0, unroll=8)
    lane_tile = lax.broadcasted_iota(jnp.int32, (1, LANES), 1) // TILE
    tiles = LANES // TILE
    for k in range(live_ref.shape[0]):
        part = jnp.full((1, LANES), tile_ref[k * tiles], F32)
        for t in range(1, tiles):
            part = jnp.where(lane_tile == t, tile_ref[k * tiles + t], part)
        live_ref[k : k + 1, :] = part

    perm_rows = perm_ref[pl.ds(row_index, 1), :] - row_index * rows
    perm_line = perm_ref[pl.ds(col_index // (rows // cols), 1), :] - col_index * cols
    perm_cols = perm_line[:, :cols]
    for k in range(1, rows // cols):
        other = perm_line[:, k * cols : (k + 1) * cols]
        perm_cols = jnp.where(lax.rem(col_index, rows // cols) == k, other, perm_cols)
    pick_rows = (lax.broadcasted_iota(jnp.int32, (rows, rows), 0) == perm_rows).astype(BF16)
    pick_cols = (lax.broadcasted_iota(jnp.int32, (cols, cols), 0) == perm_cols).astype(BF16)
    bins = bins_ref[...].astype(F32).astype(BF16)
    moved = dot(pick_rows, bins, 0, 1).astype(BF16)
    rows_ref[...] = dot(moved, pick_cols)
    target_ref[...] = jnp.concatenate(
        [rows_ref[pl.ds(k, rows // group, stride=group), :] for k in range(group)], axis=1
    )


def prepare(
    counts,
    order,
    bins,
    perm,
    gain_first,
    first_in,
    first_out,
    gain_second,
    second_in,
    second_out,
    head,
):
    cols, rows = bins.shape
    width, double = first_in.shape
    hid = first_out.shape[0]
    lines = rows * cols // LANES
    shapes = [
        ((width, double), BF16),
        ((double, width), BF16),
        ((width, hid), BF16),
        ((width, double), BF16),
        ((double, width), BF16),
        ((width, hid), BF16),
        ((width, head.shape[0]), BF16),
        ((width, 2), F32),
        ((lines, LANES), F32),
        ((lines, LANES), F32),
    ]
    small = (
        bins,
        perm,
        gain_first,
        first_in,
        first_out,
        gain_second,
        second_in,
        second_out,
        head,
    )
    return pl.pallas_call(
        prepare_kernel,
        grid_spec=pltpu.PrefetchScalarGridSpec(
            num_scalar_prefetch=2,
            grid=(1,),
            in_specs=[pl.BlockSpec(x.shape, lambda i, *_: (0, 0)) for x in small],
            out_specs=[pl.BlockSpec(shape, lambda i, *_: (0, 0)) for shape, _ in shapes],
            scratch_shapes=[
                pltpu.SMEM((rows * cols // TILE,), F32),
                pltpu.VMEM((rows, cols), F32),
            ],
        ),
        out_shape=[jax.ShapeDtypeStruct(shape, dtype) for shape, dtype in shapes],
        compiler_params=pltpu.CompilerParams(vmem_limit_bytes=VMEM_LIMIT),
        cost_estimate=pl.CostEstimate(
            flops=1 << 30, bytes_accessed=4 << 20, transcendentals=0
        ),
    )(counts, order, *small)


def pair_kernel(
    tokens,
    pair_ref,
    left_ref,
    right_ref,
    first_out_ref,
    second_out_ref,
    head_turned,
    first_half,
    first_in_turned,
    first_out_turned,
    second_half,
    second_in_turned,
    second_out_turned,
    head_ref,
    gains_ref,
    live_ref,
    target_ref,
    pair_grad_ref,
    buffer_ref,
    right_grad_ref,
    act_one,
    slope_one,
    act_two,
    slope_two,
    hidden_two,
    both_two,
    in_sum,
    out_sum,
    head_sum,
    right_sum,
):
    block_rows, cols, width = pair_ref.shape
    pairs = block_rows * cols
    hid = first_out_ref.shape[0]
    step = pl.program_id(0)
    vectors = pairs // LANES
    blocks, depth, _ = buffer_ref.shape
    own_rows = pl.num_programs(0) * block_rows // blocks
    share = depth - max(own_rows, 16)

    @pl.when(step == 0)
    def _():
        right_sum[...] = jnp.zeros_like(right_sum)
        in_sum[...] = jnp.zeros_like(in_sum)
        out_sum[...] = jnp.zeros_like(out_sum)
        head_sum[...] = jnp.zeros_like(head_sum)
        buffer_ref[...] = jnp.zeros_like(buffer_ref)

    def flow(part_index):
        part_pairs = pairs // PARTS
        part_vectors = vectors // PARTS
        lanes = slice(part_index * part_pairs, (part_index + 1) * part_pairs)
        part_rows = slice(
            part_index * (block_rows // PARTS), (part_index + 1) * (block_rows // PARTS)
        )
        field = pair_ref[part_rows].astype(F32) + left_ref[part_rows, :width][:, None, :]
        field = (field + right_ref[...].astype(F32)[None]).reshape(part_pairs, width)
        field = jnp.transpose(field)
        yield
        normed_one, scaling_one = norm(field)
        inputs_one = (normed_one * gains_ref[:, 0:1]).astype(BF16)
        yield
        delta_one = yield from forward(
            inputs_one, first_in_turned, first_out_turned, act_one, slope_one, None, lanes
        )
        yield
        pair_one = (field + delta_one).astype(BF16).astype(F32)

        normed_two, scaling_two = norm(pair_one)
        inputs_two = (normed_two * gains_ref[:, 1:2]).astype(BF16)
        yield
        delta_two = yield from forward(
            inputs_two, second_in_turned, second_out_turned, act_two, slope_two, hidden_two, lanes
        )
        yield
        line = step * vectors + part_index * part_vectors
        live = jnp.concatenate(
            [live_ref[pl.ds(line + k, 1), :] for k in range(part_vectors)], axis=1
        )
        pair_two = (pair_one + live * delta_two).astype(BF16)

        logits = dot(head_turned[...], pair_two)
        yield
        exponent = jnp.exp(logits - jnp.max(logits, axis=0, keepdims=True))
        probability = exponent * (1.0 / jnp.sum(exponent, axis=0, keepdims=True))
        target = jnp.concatenate(
            [target_ref[pl.ds(line + k, 1), :] for k in range(part_vectors)], axis=1
        ).astype(jnp.int32)
        onehot = lax.broadcasted_iota(jnp.int32, logits.shape, 0) == target
        grad_logits = (probability - onehot.astype(F32)).astype(BF16)
        yield
        grad_two = dot(head_ref[...], grad_logits).astype(BF16).astype(F32)
        head_sum[...] += dot(grad_logits, pair_two, 1, 1)

        grad_delta = (grad_two * live).astype(BF16)
        yield
        back_two = yield from backward(
            grad_delta,
            normed_two,
            scaling_two,
            gains_ref[:, 1:2],
            second_half,
            second_out_ref,
            act_two,
            slope_two,
            both_two,
            lanes,
        )
        in_sum[...] += dot(inputs_two, both_two[:, lanes], 1, 1)
        out_sum[...] += dot(grad_delta, hidden_two[:, lanes], 1, 1)
        yield

        grad_one = (grad_two + back_two).astype(BF16)
        back_one = yield from backward(
            grad_one,
            normed_one,
            scaling_one,
            gains_ref[:, 0:1],
            first_half,
            first_out_ref,
            act_one,
            slope_one,
            None,
            lanes,
        )
        yield
        grad_zero = jnp.transpose(grad_one.astype(F32) + back_one).reshape(-1, cols, width)
        pair_grad_ref[part_rows] = grad_zero.astype(BF16)
        right_sum[...] += jnp.sum(grad_zero, axis=0)
        left_grad = jnp.sum(grad_zero, axis=1).astype(BF16)
        per_part = block_rows // PARTS // own_rows
        per_step = block_rows // own_rows
        for k in range(per_part):
            part = left_grad[k * own_rows : (k + 1) * own_rows]
            buffer_ref[step * per_step + part_index * per_part + k, share : share + own_rows, :] = part

    flows = [flow(k) for k in range(PARTS)]
    for k, each in enumerate(flows):
        for _ in range((PARTS - 1 - k) * AHEAD):
            next(each)
    while flows:
        for each in list(flows):
            if next(each, flows) is flows:
                flows.remove(each)

    @pl.when(step == pl.num_programs(0) - 1)
    def _():
        scale = 1.0 / tokens
        right_grad_ref[...] = right_sum[...].astype(BF16)
        parts = []
        for j in range(0, 2 * hid, width):
            factor = scale * 0.5 if j < hid else scale
            parts.append((in_sum[:, j : j + width] * factor).astype(BF16))
        for j in range(0, hid, width):
            parts.append((jnp.transpose(out_sum[:, j : j + width]) * scale).astype(BF16))
        parts.append((head_sum[...] * scale).astype(BF16))
        first = 0
        for part in parts:
            for block, offset, start, stop in pieces(first, part.shape[0], share):
                buffer_ref[block, offset : offset + stop - start, :] = part[start:stop]
            first += part.shape[0]


def pieces(first, count, share):
    found, at = [], first
    while at < first + count:
        stop = min(first + count, (at // share + 1) * share)
        found.append((at // share, at % share, at - first, stop - first))
        at = stop
    return found


def unpack_kernel(share, gathered_ref, proj_ref, in_ref, out_ref, head_ref, single_ref):
    width, double = in_ref.shape
    cols = gathered_ref.shape[1] - share
    blocks = gathered_ref.shape[0]
    rows = single_ref.shape[1]
    own_rows = rows // blocks
    cols -= max(own_rows, 16)

    def put(first, count, ref, row, col):
        for block, offset, start, stop in pieces(first, count, share):
            part = gathered_ref[block, offset : offset + stop - start, :].astype(F32)
            ref[row + start : row + stop, col : col + width] = part

    for j in range(0, double, width):
        put(j, width, in_ref, 0, j)
    put(double, out_ref.shape[0], out_ref, 0, 0)
    put(double + out_ref.shape[0], head_ref.shape[0], head_ref, 0, 0)
    at = share + cols
    left = jnp.concatenate(
        [gathered_ref[b, at : at + own_rows, :].astype(F32) for b in range(blocks)], axis=0
    ).astype(BF16)
    ratio = rows // cols
    first = lax.axis_index("row") * ratio
    right = jnp.concatenate(
        [gathered_ref[first + k, share : share + cols, :] for k in range(ratio)], axis=0
    )
    single = dot(proj_ref[:, :width], left, 1, 1)
    single_ref[...] = single + dot(proj_ref[:, width:], right, 1, 1)


def unpack(gathered, proj_weight, hid, bins, rows, share):
    width = gathered.shape[2]
    shapes = [(width, 2 * hid), (hid, width), (bins, width), (proj_weight.shape[0], rows)]
    vmem = pl.BlockSpec(memory_space=pltpu.VMEM)
    return pl.pallas_call(
        functools.partial(unpack_kernel, share),
        in_specs=[vmem, vmem],
        out_specs=[vmem] * 4,
        out_shape=[jax.ShapeDtypeStruct(shape, F32) for shape in shapes],
        compiler_params=pltpu.CompilerParams(vmem_limit_bytes=16 << 20),
    )(gathered, proj_weight)


def pair_grid(
    pair_in,
    projected,
    right_part,
    first_out,
    second_out,
    head_turned,
    prepared,
    tokens,
    n_col,
    share,
):
    rows, cols, width = pair_in.shape
    block_rows = min(BLOCK_ROWS, rows)
    pairs = block_rows * cols
    hid = first_out.shape[0]
    bins = head_turned.shape[0]
    depth = share + max(rows // n_col, 16)

    def whole(x):
        return pl.BlockSpec(x.shape, lambda i: (0,) * x.ndim)

    def fixed(*shape):
        return pl.BlockSpec(shape, lambda i: (0,) * len(shape))

    small = (right_part, first_out, second_out, head_turned, *prepared)
    macs = rows * cols * width * (16 * hid + 3 * bins)
    return pl.pallas_call(
        functools.partial(pair_kernel, tokens),
        grid=(rows // block_rows,),
        in_specs=[
            pl.BlockSpec((block_rows, cols, width), lambda i: (i, 0, 0)),
            pl.BlockSpec((block_rows, projected.shape[1]), lambda i: (i, 0)),
        ]
        + [whole(x) for x in small],
        out_specs=[
            pl.BlockSpec((block_rows, cols, width), lambda i: (i, 0, 0)),
            fixed(n_col, depth, width),
            fixed(cols, width),
        ],
        scratch_shapes=[
            pltpu.VMEM((hid, pairs), BF16),
            pltpu.VMEM((hid, pairs), BF16),
            pltpu.VMEM((hid, pairs), BF16),
            pltpu.VMEM((hid, pairs), BF16),
            pltpu.VMEM((hid, pairs), BF16),
            pltpu.VMEM((2 * hid, pairs), BF16),
            pltpu.VMEM((width, 2 * hid), F32),
            pltpu.VMEM((width, hid), F32),
            pltpu.VMEM((bins, width), F32),
            pltpu.VMEM((cols, width), F32),
        ],
        out_shape=[
            jax.ShapeDtypeStruct((rows, cols, width), BF16),
            pltpu.VMEM((n_col, depth, width), BF16),
            pltpu.VMEM((cols, width), BF16),
        ],
        compiler_params=pltpu.CompilerParams(
            vmem_limit_bytes=VMEM_LIMIT, dimension_semantics=("arbitrary",)
        ),
        cost_estimate=pl.CostEstimate(
            flops=2 * macs,
            bytes_accessed=4 * rows * cols * width,
            transcendentals=2 * rows * cols * hid,
        ),
    )(pair_in, projected, *small)


def swap(x, axis, size, mask):
    return lax.ppermute(x, axis, [(i, i ^ mask) for i in range(size)])


def tree_sum(parts):
    parts = [p.astype(F32) for p in parts]
    while len(parts) > 1:
        parts = [parts[k] + parts[k + 1] for k in range(0, len(parts), 2)]
    return parts[0]


def local(
    n_row,
    n_col,
    singles,
    pair_in,
    proj_weight,
    gain_first,
    first_in,
    first_out,
    gain_second,
    second_in,
    second_out,
    head_weight,
    pae_bins,
    chain_perm,
    resolved_counts,
    tile_order,
):
    rows, cols, width = pair_in.shape
    tokens = chain_perm.shape[0]
    hid = first_out.shape[0]
    bins = head_weight.shape[1]
    col_index = lax.axis_index("col")
    ratio = rows // cols

    joined = jnp.concatenate([singles.T, proj_weight], axis=1)
    joined = lax.all_gather(joined, "col", axis=0, tiled=True)
    projected = dot(joined[:, :rows], joined[:, rows:], 0, 0)
    own_half = lax.dynamic_slice_in_dim(
        projected[:, width:], (col_index % ratio) * cols, cols, 0
    ).astype(BF16)
    right_part = lax.ppermute(
        own_half,
        ("row", "col"),
        [
            ((c // ratio) * n_col + z * ratio + c % ratio, z * n_col + c)
            for z in range(n_row)
            for c in range(n_col)
        ],
    )
    head_turned = head_weight.T
    prepared = prepare(
        resolved_counts,
        tile_order,
        pae_bins.T,
        chain_perm.reshape(n_row, rows),
        gain_first.reshape(1, width),
        first_in,
        first_out,
        gain_second.reshape(1, width),
        second_in,
        second_out,
        head_turned,
    )

    share = -(-(3 * hid + bins) // (n_col * 16)) * 16
    pair_grad, buffer, right_grad = pair_grid(
        pair_in,
        projected,
        right_part,
        first_out,
        second_out,
        head_turned,
        prepared,
        tokens,
        n_col,
        share,
    )

    buffer = lax.all_to_all(buffer, "col", 0, 0, tiled=True)
    buffer = tree_sum([buffer[k] for k in range(n_col)]).astype(BF16)
    own = jnp.concatenate([buffer[:share], right_grad], axis=0)
    own = tree_sum([own] + [swap(own, "row", n_row, k) for k in range(1, n_row)]).astype(BF16)
    own = jnp.concatenate([own, buffer[share:]], axis=0)
    gathered = lax.all_gather(own, "col", axis=0)
    in_grad, out_grad, head_grad, single_grad = unpack(
        gathered, proj_weight, hid, bins, rows, share
    )
    return pair_grad, single_grad.T, in_grad, out_grad, head_grad.T


def solution(mesh):
    in_specs = (
        P("row", "col"),
        P("row", "col", None),
        P("col", None),
        P(),
        P(),
        P(),
        P(),
        P(),
        P(),
        P(),
        P("row", "col"),
        P(),
        P("row", None),
        P("row", "col"),
    )
    out_specs = (P("row", "col", None), P("row", "col"), P(), P(), P())
    return jax.shard_map(
        functools.partial(local, mesh.shape["row"], mesh.shape["col"]),
        mesh=mesh,
        in_specs=in_specs,
        out_specs=out_specs,
        check_vma=False,
    )
```

```python
import functools

import jax
import jax.numpy as jnp
from jax import lax
from jax.experimental import pallas as pl
from jax.experimental.pallas import tpu as pltpu
from jax.sharding import PartitionSpec as P

TILE = 32
LANES = 128
BLOCK_ROWS = 64
CHUNK = 256
VMEM_LIMIT = 61 << 20
PARTS = 2
AHEAD = 2
F32 = jnp.float32
BF16 = jnp.bfloat16


def dot(left_op, right_op, left_dim=1, right_dim=0):
    return lax.dot_general(
        left_op,
        right_op,
        (((left_dim,), (right_dim,)), ((), ())),
        preferred_element_type=F32,
    )


def norm(field):
    centred = field - jnp.mean(field, axis=0, keepdims=True)
    scaling = lax.rsqrt(jnp.mean(centred * centred, axis=0, keepdims=True) + 1e-05)
    return centred * scaling, scaling


def forward(inputs, in_turned, out_turned, act_ref, slope_ref, hidden_ref, lanes):
    hid = out_turned.shape[1]
    result = None
    for j in range(0, hid, CHUNK):
        half_gate = dot(in_turned[j : j + CHUNK, :], inputs).astype(BF16)
        up = dot(in_turned[hid + j : hid + j + CHUNK, :], inputs).astype(BF16)
        yield
        twice_sig = 1.0 + jnp.tanh(half_gate)
        act = half_gate * twice_sig
        hidden = act * up
        act_ref[j : j + CHUNK, lanes] = act
        slope_ref[j : j + CHUNK, lanes] = up * (twice_sig + act * (2.0 - twice_sig))
        if hidden_ref is not None:
            hidden_ref[j : j + CHUNK, lanes] = hidden
        yield
        part = dot(out_turned[:, j : j + CHUNK], hidden)
        result = part if result is None else result + part
    return result


def backward(grad_out, normed, scaling, gain, w_in, w_out, act_ref, slope_ref, both_ref, lanes):
    hid = w_out.shape[0]
    grad_normed = None
    for j in range(0, hid, CHUNK):
        grad_hidden = dot(w_out[j : j + CHUNK, :], grad_out).astype(BF16)
        yield
        grad_gate = grad_hidden * slope_ref[j : j + CHUNK, lanes]
        grad_up = grad_hidden * act_ref[j : j + CHUNK, lanes]
        if both_ref is not None:
            both_ref[j : j + CHUNK, lanes] = grad_gate
            both_ref[hid + j : hid + j + CHUNK, lanes] = grad_up
        yield
        part = dot(w_in[:, j : j + CHUNK], grad_gate)
        part = part + dot(w_in[:, hid + j : hid + j + CHUNK], grad_up)
        grad_normed = part if grad_normed is None else grad_normed + part
    grad_normed = grad_normed * gain
    mean = jnp.mean(grad_normed, axis=0, keepdims=True)
    slant = jnp.mean(grad_normed * normed, axis=0, keepdims=True)
    return scaling * (grad_normed - mean - normed * slant)


def turned(x):
    return jnp.transpose(x.astype(F32)).astype(x.dtype)


def prepare_kernel(
    counts_ref,
    order_ref,
    bins_ref,
    perm_ref,
    gain_first_ref,
    first_in_ref,
    first_out_ref,
    gain_second_ref,
    second_in_ref,
    second_out_ref,
    head_ref,
    first_half,
    first_in_turned,
    first_out_turned,
    second_half,
    second_in_turned,
    second_out_turned,
    head_turned,
    gains_ref,
    live_ref,
    target_ref,
    tile_ref,
    rows_ref,
):
    cols, rows = bins_ref.shape
    hid = first_out_ref.shape[0]
    group = LANES // cols
    row_index, col_index = lax.axis_index("row"), lax.axis_index("col")
    for half, half_turned, whole in (
        (first_half, first_in_turned, first_in_ref),
        (second_half, second_in_turned, second_in_ref),
    ):
        half[:, :hid] = whole[:, :hid] * jnp.asarray(0.5, BF16)
        half[:, hid:] = whole[:, hid:]
        half_turned[...] = turned(half[...])
    first_out_turned[...] = turned(first_out_ref[...])
    second_out_turned[...] = turned(second_out_ref[...])
    head_turned[...] = turned(head_ref[...])
    gains_ref[:, 0:1] = jnp.transpose(gain_first_ref[...])
    gains_ref[:, 1:2] = jnp.transpose(gain_second_ref[...])

    count = counts_ref[0, col_index]

    def place(t, carry):
        tile_ref[order_ref[0, t]] = jnp.where(t < count, 1.0, 0.0).astype(F32)
        return carry

    lax.fori_loop(0, order_ref.shape[1], place, 0, unroll=8)
    lane_tile = lax.broadcasted_iota(jnp.int32, (1, LANES), 1) // TILE
    tiles = LANES // TILE
    for k in range(live_ref.shape[0]):
        part = jnp.full((1, LANES), tile_ref[k * tiles], F32)
        for t in range(1, tiles):
            part = jnp.where(lane_tile == t, tile_ref[k * tiles + t], part)
        live_ref[k : k + 1, :] = part

    perm_rows = perm_ref[pl.ds(row_index, 1), :] - row_index * rows
    perm_line = perm_ref[pl.ds(col_index // (rows // cols), 1), :] - col_index * cols
    perm_cols = perm_line[:, :cols]
    for k in range(1, rows // cols):
        other = perm_line[:, k * cols : (k + 1) * cols]
        perm_cols = jnp.where(lax.rem(col_index, rows // cols) == k, other, perm_cols)
    pick_rows = (lax.broadcasted_iota(jnp.int32, (rows, rows), 0) == perm_rows).astype(BF16)
    pick_cols = (lax.broadcasted_iota(jnp.int32, (cols, cols), 0) == perm_cols).astype(BF16)
    bins = bins_ref[...].astype(F32).astype(BF16)
    moved = dot(pick_rows, bins, 0, 1).astype(BF16)
    rows_ref[...] = dot(moved, pick_cols)
    target_ref[...] = jnp.concatenate(
        [rows_ref[pl.ds(k, rows // group, stride=group), :] for k in range(group)], axis=1
    )


def prepare(
    counts,
    order,
    bins,
    perm,
    gain_first,
    first_in,
    first_out,
    gain_second,
    second_in,
    second_out,
    head,
):
    cols, rows = bins.shape
    width, double = first_in.shape
    hid = first_out.shape[0]
    lines = rows * cols // LANES
    shapes = [
        ((width, double), BF16),
        ((double, width), BF16),
        ((width, hid), BF16),
        ((width, double), BF16),
        ((double, width), BF16),
        ((width, hid), BF16),
        ((width, head.shape[0]), BF16),
        ((width, 2), F32),
        ((lines, LANES), F32),
        ((lines, LANES), F32),
    ]
    small = (
        bins,
        perm,
        gain_first,
        first_in,
        first_out,
        gain_second,
        second_in,
        second_out,
        head,
    )
    return pl.pallas_call(
        prepare_kernel,
        grid_spec=pltpu.PrefetchScalarGridSpec(
            num_scalar_prefetch=2,
            grid=(1,),
            in_specs=[pl.BlockSpec(x.shape, lambda i, *_: (0, 0)) for x in small],
            out_specs=[pl.BlockSpec(shape, lambda i, *_: (0, 0)) for shape, _ in shapes],
            scratch_shapes=[
                pltpu.SMEM((rows * cols // TILE,), F32),
                pltpu.VMEM((rows, cols), F32),
            ],
        ),
        out_shape=[jax.ShapeDtypeStruct(shape, dtype) for shape, dtype in shapes],
        compiler_params=pltpu.CompilerParams(vmem_limit_bytes=VMEM_LIMIT),
        cost_estimate=pl.CostEstimate(
            flops=1 << 30, bytes_accessed=4 << 20, transcendentals=0
        ),
    )(counts, order, *small)


def pair_kernel(
    tokens,
    pair_ref,
    left_ref,
    right_ref,
    first_out_ref,
    second_out_ref,
    head_turned,
    first_half,
    first_in_turned,
    first_out_turned,
    second_half,
    second_in_turned,
    second_out_turned,
    head_ref,
    gains_ref,
    live_ref,
    target_ref,
    pair_grad_ref,
    buffer_ref,
    right_grad_ref,
    act_one,
    slope_one,
    act_two,
    slope_two,
    hidden_two,
    both_two,
    in_sum,
    out_sum,
    head_sum,
    right_sum,
):
    block_rows, cols, width = pair_ref.shape
    pairs = block_rows * cols
    hid = first_out_ref.shape[0]
    step = pl.program_id(0)
    vectors = pairs // LANES
    blocks, depth, _ = buffer_ref.shape
    own_rows = pl.num_programs(0) * block_rows // blocks
    share = depth - max(own_rows, 16)

    @pl.when(step == 0)
    def _():
        right_sum[...] = jnp.zeros_like(right_sum)
        in_sum[...] = jnp.zeros_like(in_sum)
        out_sum[...] = jnp.zeros_like(out_sum)
        head_sum[...] = jnp.zeros_like(head_sum)
        buffer_ref[...] = jnp.zeros_like(buffer_ref)

    def flow(part_index):
        part_pairs = pairs // PARTS
        part_vectors = vectors // PARTS
        lanes = slice(part_index * part_pairs, (part_index + 1) * part_pairs)
        part_rows = slice(
            part_index * (block_rows // PARTS), (part_index + 1) * (block_rows // PARTS)
        )
        field = pair_ref[part_rows].astype(F32) + left_ref[part_rows, :width][:, None, :]
        field = (field + right_ref[...].astype(F32)[None]).reshape(part_pairs, width)
        field = jnp.transpose(field)
        yield
        normed_one, scaling_one = norm(field)
        inputs_one = (normed_one * gains_ref[:, 0:1]).astype(BF16)
        yield
        delta_one = yield from forward(
            inputs_one, first_in_turned, first_out_turned, act_one, slope_one, None, lanes
        )
        yield
        pair_one = (field + delta_one).astype(BF16).astype(F32)

        normed_two, scaling_two = norm(pair_one)
        inputs_two = (normed_two * gains_ref[:, 1:2]).astype(BF16)
        yield
        delta_two = yield from forward(
            inputs_two, second_in_turned, second_out_turned, act_two, slope_two, hidden_two, lanes
        )
        yield
        line = step * vectors + part_index * part_vectors
        live = jnp.concatenate(
            [live_ref[pl.ds(line + k, 1), :] for k in range(part_vectors)], axis=1
        )
        pair_two = (pair_one + live * delta_two).astype(BF16)

        logits = dot(head_turned[...], pair_two)
        yield
        exponent = jnp.exp(logits - jnp.max(logits, axis=0, keepdims=True))
        probability = exponent * (1.0 / jnp.sum(exponent, axis=0, keepdims=True))
        target = jnp.concatenate(
            [target_ref[pl.ds(line + k, 1), :] for k in range(part_vectors)], axis=1
        ).astype(jnp.int32)
        onehot = lax.broadcasted_iota(jnp.int32, logits.shape, 0) == target
        grad_logits = (probability - onehot.astype(F32)).astype(BF16)
        yield
        grad_two = dot(head_ref[...], grad_logits).astype(BF16).astype(F32)
        head_sum[...] += dot(grad_logits, pair_two, 1, 1)

        grad_delta = (grad_two * live).astype(BF16)
        yield
        back_two = yield from backward(
            grad_delta,
            normed_two,
            scaling_two,
            gains_ref[:, 1:2],
            second_half,
            second_out_ref,
            act_two,
            slope_two,
            both_two,
            lanes,
        )
        in_sum[...] += dot(inputs_two, both_two[:, lanes], 1, 1)
        out_sum[...] += dot(grad_delta, hidden_two[:, lanes], 1, 1)
        yield

        grad_one = (grad_two + back_two).astype(BF16)
        back_one = yield from backward(
            grad_one,
            normed_one,
            scaling_one,
            gains_ref[:, 0:1],
            first_half,
            first_out_ref,
            act_one,
            slope_one,
            None,
            lanes,
        )
        yield
        grad_zero = jnp.transpose(grad_one.astype(F32) + back_one).reshape(-1, cols, width)
        pair_grad_ref[part_rows] = grad_zero.astype(BF16)
        right_sum[...] += jnp.sum(grad_zero, axis=0)
        left_grad = jnp.sum(grad_zero, axis=1).astype(BF16)
        per_part = block_rows // PARTS // own_rows
        per_step = block_rows // own_rows
        for k in range(per_part):
            part = left_grad[k * own_rows : (k + 1) * own_rows]
            buffer_ref[step * per_step + part_index * per_part + k, share : share + own_rows, :] = part

    flows = [flow(k) for k in range(PARTS)]
    for k, each in enumerate(flows):
        for _ in range((PARTS - 1 - k) * AHEAD):
            next(each)
    while flows:
        for each in list(flows):
            if next(each, flows) is flows:
                flows.remove(each)

    @pl.when(step == pl.num_programs(0) - 1)
    def _():
        scale = 1.0 / tokens
        right_grad_ref[...] = right_sum[...].astype(BF16)
        parts = []
        for j in range(0, 2 * hid, width):
            factor = scale * 0.5 if j < hid else scale
            parts.append((in_sum[:, j : j + width] * factor).astype(BF16))
        for j in range(0, hid, width):
            parts.append((jnp.transpose(out_sum[:, j : j + width]) * scale).astype(BF16))
        parts.append((head_sum[...] * scale).astype(BF16))
        first = 0
        for part in parts:
            for block, offset, start, stop in pieces(first, part.shape[0], share):
                buffer_ref[block, offset : offset + stop - start, :] = part[start:stop]
            first += part.shape[0]


def pieces(first, count, share):
    found, at = [], first
    while at < first + count:
        stop = min(first + count, (at // share + 1) * share)
        found.append((at // share, at % share, at - first, stop - first))
        at = stop
    return found


def unpack_kernel(share, gathered_ref, proj_ref, in_ref, out_ref, head_ref, single_ref):
    width, double = in_ref.shape
    cols = gathered_ref.shape[1] - share
    blocks = gathered_ref.shape[0]
    rows = single_ref.shape[1]
    own_rows = rows // blocks
    cols -= max(own_rows, 16)

    def put(first, count, ref, row, col):
        for block, offset, start, stop in pieces(first, count, share):
            part = gathered_ref[block, offset : offset + stop - start, :].astype(F32)
            ref[row + start : row + stop, col : col + width] = part

    for j in range(0, double, width):
        put(j, width, in_ref, 0, j)
    put(double, out_ref.shape[0], out_ref, 0, 0)
    put(double + out_ref.shape[0], head_ref.shape[0], head_ref, 0, 0)
    at = share + cols
    left = jnp.concatenate(
        [gathered_ref[b, at : at + own_rows, :].astype(F32) for b in range(blocks)], axis=0
    ).astype(BF16)
    ratio = rows // cols
    first = lax.axis_index("row") * ratio
    right = jnp.concatenate(
        [gathered_ref[first + k, share : share + cols, :] for k in range(ratio)], axis=0
    )
    single = dot(proj_ref[:, :width], left, 1, 1)
    single_ref[...] = single + dot(proj_ref[:, width:], right, 1, 1)


def unpack(gathered, proj_weight, hid, bins, rows, share):
    width = gathered.shape[2]
    shapes = [(width, 2 * hid), (hid, width), (bins, width), (proj_weight.shape[0], rows)]
    vmem = pl.BlockSpec(memory_space=pltpu.VMEM)
    return pl.pallas_call(
        functools.partial(unpack_kernel, share),
        in_specs=[vmem, vmem],
        out_specs=[vmem] * 4,
        out_shape=[jax.ShapeDtypeStruct(shape, F32) for shape in shapes],
        compiler_params=pltpu.CompilerParams(vmem_limit_bytes=16 << 20),
    )(gathered, proj_weight)


def pair_grid(
    pair_in,
    projected,
    right_part,
    first_out,
    second_out,
    head_turned,
    prepared,
    tokens,
    n_col,
    share,
):
    rows, cols, width = pair_in.shape
    block_rows = min(BLOCK_ROWS, rows)
    pairs = block_rows * cols
    hid = first_out.shape[0]
    bins = head_turned.shape[0]
    depth = share + max(rows // n_col, 16)

    def whole(x):
        return pl.BlockSpec(x.shape, lambda i: (0,) * x.ndim)

    def fixed(*shape):
        return pl.BlockSpec(shape, lambda i: (0,) * len(shape))

    small = (right_part, first_out, second_out, head_turned, *prepared)
    macs = rows * cols * width * (16 * hid + 3 * bins)
    return pl.pallas_call(
        functools.partial(pair_kernel, tokens),
        grid=(rows // block_rows,),
        in_specs=[
            pl.BlockSpec((block_rows, cols, width), lambda i: (i, 0, 0)),
            pl.BlockSpec((block_rows, projected.shape[1]), lambda i: (i, 0)),
        ]
        + [whole(x) for x in small],
        out_specs=[
            pl.BlockSpec((block_rows, cols, width), lambda i: (i, 0, 0)),
            fixed(n_col, depth, width),
            fixed(cols, width),
        ],
        scratch_shapes=[
            pltpu.VMEM((hid, pairs), BF16),
            pltpu.VMEM((hid, pairs), BF16),
            pltpu.VMEM((hid, pairs), BF16),
            pltpu.VMEM((hid, pairs), BF16),
            pltpu.VMEM((hid, pairs), BF16),
            pltpu.VMEM((2 * hid, pairs), BF16),
            pltpu.VMEM((width, 2 * hid), F32),
            pltpu.VMEM((width, hid), F32),
            pltpu.VMEM((bins, width), F32),
            pltpu.VMEM((cols, width), F32),
        ],
        out_shape=[
            jax.ShapeDtypeStruct((rows, cols, width), BF16),
            pltpu.VMEM((n_col, depth, width), BF16),
            pltpu.VMEM((cols, width), BF16),
        ],
        compiler_params=pltpu.CompilerParams(
            vmem_limit_bytes=VMEM_LIMIT, dimension_semantics=("arbitrary",)
        ),
        cost_estimate=pl.CostEstimate(
            flops=2 * macs,
            bytes_accessed=4 * rows * cols * width,
            transcendentals=2 * rows * cols * hid,
        ),
    )(pair_in, projected, *small)


def swap(x, axis, size, mask):
    return lax.ppermute(x, axis, [(i, i ^ mask) for i in range(size)])


def tree_sum(parts):
    parts = [p.astype(F32) for p in parts]
    while len(parts) > 1:
        parts = [parts[k] + parts[k + 1] for k in range(0, len(parts), 2)]
    return parts[0]


def local(
    n_row,
    n_col,
    singles,
    pair_in,
    proj_weight,
    gain_first,
    first_in,
    first_out,
    gain_second,
    second_in,
    second_out,
    head_weight,
    pae_bins,
    chain_perm,
    resolved_counts,
    tile_order,
):
    rows, cols, width = pair_in.shape
    tokens = chain_perm.shape[0]
    hid = first_out.shape[0]
    bins = head_weight.shape[1]
    col_index = lax.axis_index("col")
    ratio = rows // cols

    joined = jnp.concatenate([singles.T, proj_weight], axis=1)
    joined = lax.all_gather(joined, "col", axis=0, tiled=True)
    projected = dot(joined[:, :rows], joined[:, rows:], 0, 0)
    own_half = lax.dynamic_slice_in_dim(
        projected[:, width:], (col_index % ratio) * cols, cols, 0
    ).astype(BF16)
    right_part = lax.ppermute(
        own_half,
        ("row", "col"),
        [
            ((c // ratio) * n_col + z * ratio + c % ratio, z * n_col + c)
            for z in range(n_row)
            for c in range(n_col)
        ],
    )
    head_turned = head_weight.T
    prepared = prepare(
        resolved_counts,
        tile_order,
        pae_bins.T,
        chain_perm.reshape(n_row, rows),
        gain_first.reshape(1, width),
        first_in,
        first_out,
        gain_second.reshape(1, width),
        second_in,
        second_out,
        head_turned,
    )

    share = -(-(3 * hid + bins) // (n_col * 16)) * 16
    pair_grad, buffer, right_grad = pair_grid(
        pair_in,
        projected,
        right_part,
        first_out,
        second_out,
        head_turned,
        prepared,
        tokens,
        n_col,
        share,
    )

    buffer = lax.all_to_all(buffer, "col", 0, 0, tiled=True)
    buffer = tree_sum([buffer[k] for k in range(n_col)]).astype(BF16)
    own = jnp.concatenate([buffer[:share], right_grad], axis=0)
    own = tree_sum([own] + [swap(own, "row", n_row, k) for k in range(1, n_row)]).astype(BF16)
    own = jnp.concatenate([own, buffer[share:]], axis=0)
    gathered = lax.all_gather(own, "col", axis=0)
    in_grad, out_grad, head_grad, single_grad = unpack(
        gathered, proj_weight, hid, bins, rows, share
    )
    return pair_grad, single_grad.T, in_grad, out_grad, head_grad.T


def solution(mesh):
    in_specs = (
        P("row", "col"),
        P("row", "col", None),
        P("col", None),
        P(),
        P(),
        P(),
        P(),
        P(),
        P(),
        P(),
        P("row", "col"),
        P(),
        P("row", None),
        P("row", "col"),
    )
    out_specs = (P("row", "col", None), P("row", "col"), P(), P(), P())
    return jax.shard_map(
        functools.partial(local, mesh.shape["row"], mesh.shape["col"]),
        mesh=mesh,
        in_specs=in_specs,
        out_specs=out_specs,
        check_vma=False,
    )
```
